32 devices in a mesh: groups: 2 (over y), expert: 4 (over z), fsdp: 2 (over x), ctx: 2 (over core).
Axes of the slice: x: 2, y: 2, z: 4, core: 2. Of those that a mesh axis runs over, the one named last changes fastest.
Arguments:
- inputs: bfloat16 [4, 1024, 2048], P(('groups', 'fsdp'), ('expert', 'ctx')), parts along dimension 0, may hold values from -6 to 6
- queries: bfloat16 [4, 1024, 2048], P(('groups', 'fsdp'), ('expert', 'ctx')), parts along dimension 0, may hold values from -131 to 131
- keys: bfloat16 [4, 1024, 2048], P(('groups', 'fsdp'), ('expert', 'ctx')), parts along dimension 0, may hold values from -5.1 to 5.1
- values: bfloat16 [4, 1024, 2048], P(('groups', 'fsdp'), ('expert', 'ctx')), parts along dimension 0, may hold values from -6 to 6
- doc_ids: int32 [4, 1024], P(('groups', 'fsdp')), parts along dimension 0, may hold values from 0 to 11, never falling along the last dimension, each value on 1 to 128 neighbouring positions
- norm_gain: float32 [2048], replicated, may hold values from 0.1 to 1.9
- expert_ids: int32 [4, 1024, 2], P(('groups', 'fsdp'), ('expert', 'ctx')), parts along dimension 0, may hold values from 0 to 3, all different within a row; in each aligned block of 128 rows (0 to 127, 128 to 255, ..., all dimensions but the last counted through in order) at most 80 rows name the same one
- gate_weights: float32 [4, 1024, 2], P(('groups', 'fsdp'), ('expert', 'ctx')), parts along dimension 0, may hold values from 0.1 to 0.9
- w_gate: bfloat16 [4, 2048, 768], P('expert', ('fsdp', 'ctx')), may hold values from -0.125 to 0.125
- w_up: bfloat16 [4, 2048, 768], P('expert', ('fsdp', 'ctx')), may hold values from -0.125 to 0.125
- w_down: bfloat16 [4, 768, 2048], P('expert', None, ('fsdp', 'ctx')), may hold values from -0.21875 to 0.21875
- out_grad: bfloat16 [4, 1024, 2048], P(('groups', 'fsdp'), ('expert', 'ctx')), parts along dimension 0, may hold values from -6 to 6
Outputs:
- layer_out: bfloat16 [4, 1024, 2048], P(('groups', 'fsdp'), ('expert', 'ctx')), parts along dimension 0
- input_grad: bfloat16 [4, 1024, 2048], P(('groups', 'fsdp'), ('expert', 'ctx')), parts along dimension 0
The draws below stay inside these ranges and needn't reach their ends.
There are 2 independent parts, one for each index of `groups`. The reference program is written for one: setup_inputs(seed, part) draws one part's arguments, and reference() takes and returns one part's arrays. A program takes and returns all parts, laid end to end along the dimension named above; an argument that names none is the same for every part. Nothing has to cross between parts.
Inputs may be any that keep to these rules, and one draw needn't show every extreme that they name: `expert_ids`: in each aligned block of 128 positions (the positions of one device) no expert is named by more than 80 of the block's choices, and in every draw some block names some expert exactly 80 times; the two experts of a position differ. `doc_ids`: along a packed row document numbers never fall; every document has 1 to 128 positions, and some document has exactly 128.
All inputs are finite; a program needn't handle non-finite values.
Results may differ from the reference program's by a relative error of at most 0.0085.
Values may be sent and summed in bfloat16 or wider, within the bound.
No kernel may reach another device: no remote copies, remote signals or barrier semaphores. Data moves between devices by JAX's collectives and lax.ppermute only.
A program may use at most 64 MiB of HBM per device.

```python
import math
import jax
import jax.numpy as jnp
import numpy as np
from jax import lax

HEADS = 16
HD = 128
D = 2048
FF = 768
EXPERTS = 4
TOK_DEV = 128
LENGTH = 1024
ROWS = 2
CAP = 80
N_EXPERT = 4
N_FSDP = 2
N_CTX = 2


def shared_base(key):
    return jnp.clip(jax.random.normal(key, (ROWS, LENGTH, D), jnp.float32), -5.0, 5.0)


def draw_keys(key, part):
    base = shared_base(key)
    return base.astype(jnp.bfloat16)


def draw_queries(key, part):
    key = jax.random.fold_in(key, 3)
    return jnp.clip(jax.random.normal(key, (ROWS, LENGTH, D), jnp.float32), -5.0, 5.0).astype(jnp.bfloat16)


def block_levels(key, extent, cuts, least, largest):
    gain, own = 1.0, jax.random.fold_in(key, 6)
    for position, parts in cuts:
        steps = jnp.exp(jax.random.uniform(jax.random.fold_in(own, position), (parts,), jnp.float32, least / len(cuts), largest / len(cuts)))
        gain = gain * jnp.repeat(steps, extent[position] // parts).reshape([-1 if axis == position else 1 for axis in range(len(extent))])
    return gain


def length_profile(number_of, total, most, lean):
    loads = [(1 << 20) // math.isqrt(grade ** lean) + 1 for grade in range(2, number_of + 1)]
    spare, given = total - most - (number_of - 1), [1] * (number_of - 1)
    while spare > 0:
        candidates = [i for i in range(number_of - 1) if given[i] < most]
        mass, remaining = sum([loads[i] for i in candidates]), spare
        for i in candidates:
            extra = min(most - given[i], max(1, remaining * loads[i] // mass), spare)
            given[i] = given[i] + extra
            spare = spare - extra
    return np.array([most] + given)


def uneven_parts(stream_key, number_of, total, reach, skew):
    if number_of == 2:
        one = jax.random.randint(stream_key, (), max(1, total - reach), min(reach, total - 1) + 1)
        return jnp.stack([one, total - one])
    lengths = jnp.asarray(length_profile(number_of, total, reach, skew), jnp.int32)
    couples = (number_of - 1) // 2
    donor, sink = lengths[1:1 + 2 * couples:2], lengths[2:2 + 2 * couples:2]
    room = jnp.minimum(donor - 1, reach - sink)
    passed = jax.random.randint(jax.random.fold_in(stream_key, 1), (couples,), 0, 1 << 20) % (room + 1)
    lengths = lengths.at[1:1 + 2 * couples:2].set(donor - passed).at[2:2 + 2 * couples:2].set(sink + passed)
    return lengths[jax.random.permutation(jax.random.fold_in(stream_key, 2), number_of)]


def assign_block(rng, own, number, rows, count, top, limit, skew):
    sequence = jax.random.permutation(rng, count)
    crowded, usual = load_shares(count, rows * top, limit, skew, True), load_shares(count, rows * top, limit, skew, False)
    places = jnp.arange(count)

    def named(tallies, offset_by):
        used = int((tallies > 0).sum())
        fixed = max(1, used // 4)
        moved = fixed + (places - fixed + offset_by * (used - fixed)) % max(1, count - fixed)
        return jnp.zeros((count,), jnp.int32).at[sequence[jnp.where(places < fixed, places, moved)]].set(jnp.asarray(tallies, jnp.int32))

    tallies = jnp.where(number % 4 == 0, named(crowded, number // 4), named(usual, number - number // 4 - 1))
    mixed = jax.random.permutation(jax.random.fold_in(own, 3), count)
    donor, sink = mixed[0:count // 2 * 2:2], mixed[1:count // 2 * 2:2]
    slack = jnp.minimum(tallies[donor] - 1, limit - tallies[sink]) // 2
    slack = jnp.where((donor == sequence[0]) | (sink == sequence[0]) | (tallies[sink] == 0), 0, jnp.maximum(slack, 0))
    moved = jax.random.randint(jax.random.fold_in(own, 4), (count // 2,), 0, 1 << 20) % (slack + 1)
    tallies = tallies.at[donor].add(-moved).at[sink].add(moved)
    members = jnp.searchsorted(jnp.cumsum(tallies), jnp.arange(rows * top), side="right").astype(jnp.int32)
    grid = members.reshape(top, rows).T
    grid = grid[jax.random.permutation(jax.random.fold_in(own, 1), rows)]
    offset_by = jax.random.randint(jax.random.fold_in(own, 2), (rows, 1), 0, top)
    return jnp.take_along_axis(grid, (jnp.arange(top)[None, :] + offset_by) % top, axis=1)


def load_shares(count, total, bound, slope, full):
    portions = [(1 << 20) // math.isqrt(standing ** slope) + 1 for standing in range(1, count + 1)]
    largest = bound if full else min(bound, max(-(-total // count), total * portions[0] // sum(portions)))
    least = 1 if total - largest >= count - 1 else 0
    given, surplus = [largest] + [least] * (count - 1), total - largest - least * (count - 1)
    while surplus > 0:
        candidates = [i for i in range(1, count) if given[i] < largest] or [i for i in range(1, count) if given[i] < bound]
        whole, left = sum([portions[i] for i in candidates]), surplus
        for i in candidates:
            addition = min(bound - given[i], max(1, left * portions[i] // whole), surplus)
            given[i] = given[i] + addition
            surplus = surplus - addition
    return np.array(given)


def gaussian(key, extent, deviation, reach, split=(), kind=jnp.bfloat16):
    drawn = jax.random.normal(key, extent, jnp.float32) * deviation
    if len(split) > 0:
        drawn = block_levels(key, extent, split, -0.22, 0.18) * drawn
    return jnp.clip(drawn, min=-reach, max=reach).astype(kind)


def setup_inputs(seed: int = 0, part: int = 0) -> dict:
    seeds = jax.random.split(jax.random.key(seed), 13)
    own_keys = jax.random.split(jax.random.fold_in(seeds[12], part), 13)
    inputs = gaussian(own_keys[0], (ROWS, LENGTH, D), 1.0, 6.0, ((0, 2), (1, 8)))
    queries = draw_queries(jax.random.fold_in(jax.random.fold_in(seeds[12], part), 71), part)
    keys = draw_keys(jax.random.fold_in(jax.random.fold_in(seeds[12], part), 71), part)
    values = gaussian(own_keys[3], (ROWS, LENGTH, D), 1.0, 6.0, ((0, 2), (1, 8)))
    doc_ids = jax.vmap(lambda own: jnp.searchsorted(jnp.cumsum(uneven_parts(own, LENGTH // 80, LENGTH, TOK_DEV, 1)), jnp.arange(LENGTH), side="right"))(jax.random.split(own_keys[4], ROWS)).reshape((ROWS, LENGTH)).astype(jnp.int32)
    norm_gain = jnp.clip(1.0 + 0.18 * jax.random.normal(seeds[5], (D,), jnp.float32), 0.1, 1.9)
    expert_ids_keys = jax.random.split(jax.random.fold_in(own_keys[6], 1), ROWS * LENGTH // TOK_DEV)
    expert_ids_turns = jax.random.permutation(jax.random.fold_in(own_keys[6], 3), ROWS * LENGTH // TOK_DEV)
    expert_ids = jax.vmap(lambda own, number: assign_block(jax.random.fold_in(own_keys[6], 2), own, number, TOK_DEV, EXPERTS, 2, CAP, 2))(expert_ids_keys, expert_ids_turns).reshape((ROWS, LENGTH, 2))
    gate_weights = jnp.clip(0.1 + 0.79999997 * jax.random.uniform(own_keys[7], (ROWS, LENGTH, 2), jnp.float32) ** block_levels(own_keys[7], (ROWS, LENGTH, 2), ((0, 2), (1, 8)), -0.2, 0.2), 0.1, 0.9)
    w_gate = gaussian(seeds[8], (EXPERTS, D, FF), D ** -0.5, 0.125, ((0, 4), (1, 4)))
    w_up = gaussian(seeds[9], (EXPERTS, D, FF), D ** -0.5, 0.125, ((0, 4), (1, 4)))
    w_down = gaussian(seeds[10], (EXPERTS, FF, D), FF ** -0.5, 0.21875, ((0, 4), (2, 4)))
    out_grad = gaussian(own_keys[11], (ROWS, LENGTH, D), 1.0, 6.0, ((0, 2), (1, 8)))
    return {"inputs": inputs, "queries": queries, "keys": keys, "values": values, "doc_ids": doc_ids, "norm_gain": norm_gain, "expert_ids": expert_ids, "gate_weights": gate_weights, "w_gate": w_gate, "w_up": w_up, "w_down": w_down, "out_grad": out_grad}


def attend_block(query_rows, key_rows, value_rows, query_docs, key_docs):
    query_count = query_rows.shape[0]
    query_heads = query_rows.reshape(query_count, HEADS, HD).astype(jnp.float32)
    key_heads = key_rows.reshape(2 * query_count, HEADS, HD).astype(jnp.float32)
    value_heads = value_rows.reshape(2 * query_count, HEADS, HD).astype(jnp.float32)
    scores = jnp.einsum('qhd,khd->hqk', query_heads, key_heads) * HD ** (-0.5)
    query_pos = jnp.arange(query_count, dtype=jnp.int32)
    key_pos = jnp.arange(2 * query_count, dtype=jnp.int32) - query_count
    visible = (query_docs[:, None] == key_docs[None, :]) & (key_pos[None, :] <= query_pos[:, None])
    scores = jnp.where(visible[None], scores, -jnp.inf)
    row_max = lax.optimization_barrier(jnp.max(scores, axis=-1, keepdims=True))
    exp_scores = jnp.exp(scores - row_max)
    probs = (exp_scores / lax.optimization_barrier(jnp.sum(exp_scores, axis=-1, keepdims=True))).astype(jnp.bfloat16)
    result = jnp.einsum('hqk,khd->qhd', probs.astype(jnp.float32), value_heads)
    return result.reshape(query_count, HEADS * HD).astype(jnp.bfloat16)

def expert_rows(rows_in, rows_grad, gate_mat, up_mat, down_mat):
    gate_pre = jnp.dot(rows_in, gate_mat, preferred_element_type=jnp.float32)
    up_pre = jnp.dot(rows_in, up_mat, preferred_element_type=jnp.float32)
    sigmoid_val = 1.0 / (1.0 + jnp.exp(-gate_pre))
    silu_val = gate_pre * sigmoid_val
    hidden = (silu_val * up_pre).astype(jnp.bfloat16)
    expert_out = jnp.dot(hidden, down_mat, preferred_element_type=jnp.float32).astype(jnp.bfloat16)
    contract = (((1,), (1,)), ((), ()))
    hidden_grad = lax.dot_general(rows_grad, down_mat, contract, preferred_element_type=jnp.float32)
    gate_grad = (hidden_grad * up_pre * sigmoid_val * (1.0 + gate_pre * (1.0 - sigmoid_val))).astype(jnp.bfloat16)
    up_grad = (hidden_grad * silu_val).astype(jnp.bfloat16)
    partial_value = lax.dot_general(gate_grad, gate_mat, contract, preferred_element_type=jnp.float32)
    partial_value = partial_value + lax.dot_general(up_grad, up_mat, contract, preferred_element_type=jnp.float32)
    return (expert_out, partial_value.astype(jnp.bfloat16))

def attend_row(operands):
    query_row, key_row, value_row, doc_row = operands
    block_total = LENGTH // TOK_DEV
    key_pad = jnp.concatenate([jnp.zeros((TOK_DEV, D), jnp.bfloat16), key_row], 0)
    value_pad = jnp.concatenate([jnp.zeros((TOK_DEV, D), jnp.bfloat16), value_row], 0)
    doc_row = doc_row.astype(jnp.int32)
    doc_pad = jnp.concatenate([jnp.full((TOK_DEV,), -1, jnp.int32), doc_row], 0)

    def one_block(block_id):
        first_pos = (block_id * TOK_DEV).astype(jnp.int32)
        query_rows = lax.dynamic_slice_in_dim(query_row, first_pos, TOK_DEV, 0)
        key_rows = lax.dynamic_slice_in_dim(key_pad, first_pos, 2 * TOK_DEV, 0)
        value_rows = lax.dynamic_slice_in_dim(value_pad, first_pos, 2 * TOK_DEV, 0)
        query_docs = lax.dynamic_slice_in_dim(doc_row, first_pos, TOK_DEV, 0)
        key_docs = lax.dynamic_slice_in_dim(doc_pad, first_pos, 2 * TOK_DEV, 0)
        return attend_block(query_rows, key_rows, value_rows, query_docs, key_docs)
    blocks = lax.map(one_block, jnp.arange(block_total, dtype=jnp.int32))
    return blocks.reshape(LENGTH, D)

def reference(inputs, queries, keys, values, doc_ids, norm_gain, expert_ids, gate_weights, w_gate, w_up, w_down, out_grad):
    attended = lax.map(attend_row, (queries, keys, values, doc_ids))
    resid = inputs.astype(jnp.float32) + attended.astype(jnp.float32)
    inv_rms = lax.rsqrt(lax.optimization_barrier(jnp.mean(resid * resid, axis=-1, keepdims=True)) + 1e-06)
    normed = (resid * inv_rms * norm_gain).astype(jnp.bfloat16)
    token_total = ROWS * LENGTH
    flat_in = jnp.concatenate([normed.reshape(token_total, D), jnp.zeros((1, D), jnp.bfloat16)], 0)
    flat_grad = jnp.concatenate([out_grad.reshape(token_total, D), jnp.zeros((1, D), jnp.bfloat16)], 0)
    chosen = expert_ids.reshape(-1).astype(jnp.int32)
    onehot = (chosen[:, None] == jnp.arange(EXPERTS, dtype=jnp.int32)[None, :]).astype(jnp.int32)
    slot_rank = lax.optimization_barrier(jnp.sum((jnp.cumsum(onehot, axis=0).astype(jnp.int32) - onehot) * onehot, axis=1)).astype(jnp.int32)
    most_rows = N_EXPERT * N_FSDP * N_CTX * CAP
    slot_table = jnp.full((EXPERTS, most_rows), 2 * token_total, jnp.int32)
    slot_table = slot_table.at[chosen, slot_rank].set(jnp.arange(2 * token_total, dtype=jnp.int32))
    route_weight = jnp.concatenate([gate_weights.reshape(-1).astype(jnp.float32), jnp.zeros((1,), jnp.float32)], 0)

    def add_expert(totals, expert):
        out_sum, grad_sum = totals
        slot_ids = slot_table[expert]
        token_ids = (slot_ids // 2).astype(jnp.int32)
        expert_out, part_grad = expert_rows(flat_in[token_ids], flat_grad[token_ids], w_gate[expert], w_up[expert], w_down[expert])
        scaled = route_weight[slot_ids][:, None]
        out_sum = out_sum.at[token_ids].add(scaled * expert_out.astype(jnp.float32))
        grad_sum = grad_sum.at[token_ids].add(scaled * part_grad.astype(jnp.float32))
        return ((out_sum, grad_sum), None)
    zeros_acc = jnp.zeros((token_total + 1, D), jnp.float32)
    (out_sum, grad_sum), _ = lax.scan(add_expert, (zeros_acc, zeros_acc), jnp.arange(EXPERTS, dtype=jnp.int32))
    mixture = out_sum[:token_total].reshape(ROWS, LENGTH, D)
    layer_out = (resid + mixture).astype(jnp.bfloat16)
    normed_grad = grad_sum[:token_total].reshape(ROWS, LENGTH, D)
    gained = norm_gain * normed_grad
    input_grad = out_grad.astype(jnp.float32) + inv_rms * gained - resid * inv_rms ** 3 * lax.optimization_barrier(jnp.mean(resid * gained, axis=-1, keepdims=True))
    return (layer_out, input_grad.astype(jnp.bfloat16))
```

```python
import jax
import jax.numpy as jnp
from jax import lax
from jax.experimental import pallas as pl
from jax.experimental.pallas import tpu as pltpu
from jax.sharding import PartitionSpec as P

HEADS = 16
HD = 128
BF = jnp.bfloat16
F32 = jnp.float32
VM = pl.BlockSpec(memory_space=pltpu.VMEM)
ANY = pl.BlockSpec(memory_space=pl.ANY)
MIB = 1024 * 1024


def params(mib):
    return pltpu.CompilerParams(vmem_limit_bytes=mib * MIB)


def swapped(block, axis, distance):
    count = lax.axis_size(axis)
    return lax.ppermute(block, axis, [(i, i ^ distance) for i in range(count)])


def shifted(block, axis, distance):
    devices = range(lax.axis_size(axis))
    route = [(i - distance, i) for i in devices if i - distance in devices]
    return lax.ppermute(block, axis, route)


def dot(a, b):
    return jnp.dot(a, b, preferred_element_type=F32)


def dot_t(a, b):
    return lax.dot_general(a, b, (((1,), (1,)), ((), ())), preferred_element_type=F32)


def routing(ids_ref, here):
    tok = ids_ref.shape[1]
    lane = lax.broadcasted_iota(jnp.int32, (tok, 128), 1)
    row = lax.broadcasted_iota(jnp.int32, (tok, tok), 0)
    col = lax.broadcasted_iota(jnp.int32, (tok, tok), 1)
    first, second = ids_ref[0, :, 0:1] ^ here, ids_ref[0, :, 1:2] ^ here
    chosen = (first == lane) | (second == lane)
    before = (col < row).astype(BF)
    rank = dot(before, chosen.astype(BF))
    slot = jnp.where(chosen, rank, -1.0)
    return first, second, slot


def placing(slot, k, slots):
    tok = slot.shape[0]
    lane = lax.broadcasted_iota(jnp.int32, (tok, 128), 1)
    return jnp.where(lane == slot[:, k : k + 1].astype(jnp.int32), 1.0, 0.0)


def pack(rows, slot, slots, out_refs):
    places = [placing(slot, k, slots).T[:slots] for k in range(len(out_refs))]
    table = jnp.concatenate(places, 0).astype(BF)
    packed = dot(table, rows).astype(BF)
    for k, out in enumerate(out_refs):
        out[...] = packed[k * slots : (k + 1) * slots]


def pack_kernel(slots, ids_ref, rows_ref, *out_refs):
    here = lax.axis_index("expert")
    _, _, slot = routing(ids_ref, here)
    pack(rows_ref[0], slot, slots, out_refs)


def attend_kernel(
    slots, q_ref, k_ref, v_ref, kp_ref, vp_ref, doc_ref, in_ref, gain_ref, ids_ref, att_ref, *out_refs
):
    tok = q_ref.shape[1]
    here = lax.axis_index("expert")
    first = (here * lax.axis_size("ctx") + lax.axis_index("ctx")) * tok
    before = jnp.maximum(first - tok, 0)
    own_docs = doc_ref[:, pl.ds(pl.multiple_of(first, tok), tok)]
    past_docs = doc_ref[:, pl.ds(pl.multiple_of(before, tok), tok)]
    row = lax.broadcasted_iota(jnp.int32, (tok, tok), 0)
    col = lax.broadcasted_iota(jnp.int32, (tok, tok), 1)
    own_all = jnp.broadcast_to(own_docs, (tok, tok))
    query_docs = own_all.T
    see_own = (query_docs == own_all) & (col <= row)
    see_past = (query_docs == past_docs) & (first > 0)
    scale = HD ** (-0.5)
    squares = jnp.zeros((tok, HD), F32)
    for h in range(q_ref.shape[2] // HD):
        at = slice(h * HD, (h + 1) * HD)
        q = q_ref[0, :, at]
        own = jnp.where(see_own, dot_t(q, k_ref[0, :, at]) * scale, -jnp.inf)
        past = jnp.where(see_past, dot_t(q, kp_ref[0, :, at]) * scale, -jnp.inf)
        top = jnp.maximum(own, past).max(axis=1, keepdims=True)
        own, past = jnp.exp(own - top), jnp.exp(past - top)
        total = (own + past).sum(axis=1, keepdims=True)
        inverse = 1.0 / total
        own, past = (own * inverse).astype(BF), (past * inverse).astype(BF)
        part = dot(own, v_ref[0, :, at]) + dot(past, vp_ref[0, :, at])
        part = part.astype(BF)
        att_ref[:, at] = part
        resid = in_ref[0, :, at].astype(F32) + part.astype(F32)
        squares = squares + resid * resid
    width = q_ref.shape[2]
    inv_rms = lax.rsqrt(squares.sum(axis=1, keepdims=True) / width + 1e-06)
    resid = in_ref[0].astype(F32) + att_ref[...].astype(F32)
    normed = (resid * inv_rms * gain_ref[...]).astype(BF)
    _, _, slot = routing(ids_ref, here)
    pack(normed, slot, slots, out_refs)


def load_pieces(piece_refs, whole_ref, sems, axis):
    mine = lax.axis_index("fsdp") * lax.axis_size("ctx") + lax.axis_index("ctx")
    size = piece_refs[0].shape[1 + axis]
    copies = []
    for j, piece in enumerate(piece_refs):
        at = pl.ds(pl.multiple_of((mine ^ j) * size, size), size)
        target = whole_ref.at[at, :] if axis == 0 else whole_ref.at[:, at]
        copies.append(pltpu.make_async_copy(piece.at[0], target, sems.at[j]))
    for copy in copies:
        copy.start()
    return copies


def wait_all(copies):
    for copy in copies:
        copy.wait()


def forward_kernel(peers, pieces, *refs):
    rows, refs = refs[:peers], refs[peers:]
    gates, refs = refs[:pieces], refs[pieces:]
    ups, refs = refs[:pieces], refs[pieces:]
    downs, refs = refs[:pieces], refs[pieces:]
    outs, refs = refs[:peers], refs[peers:]
    slope_ref, silu_ref, gate, up, down, x, hidden, sems = refs
    copies_g = load_pieces(gates, gate, sems.at[0], 0)
    copies_u = load_pieces(ups, up, sems.at[1], 0)
    copies_d = load_pieces(downs, down, sems.at[2], 1)
    slots = rows[0].shape[0]
    for k, block in enumerate(rows):
        x[k * slots : (k + 1) * slots] = block[...]
    wait_all(copies_g)
    wait_all(copies_u)
    step = 256
    for n in range(gate.shape[1] // step):
        at = slice(n * step, (n + 1) * step)
        gate_pre = dot(x[...], gate[:, at])
        up_pre = dot(x[...], up[:, at])
        sig = 1.0 / (1.0 + jnp.exp(-gate_pre))
        silu = gate_pre * sig
        hidden[:, at] = (silu * up_pre).astype(BF)
        slope_ref[:, at] = up_pre * sig * (1.0 + gate_pre * (1.0 - sig))
        silu_ref[:, at] = silu
    wait_all(copies_d)
    step = 512
    for n in range(down.shape[1] // step):
        at = slice(n * step, (n + 1) * step)
        part = dot(hidden[...], down[:, at]).astype(BF)
        for k, out in enumerate(outs):
            out[:, at] = part[k * slots : (k + 1) * slots]


def backward_kernel(peers, pieces, *refs):
    rows, refs = refs[:peers], refs[peers:]
    gates, refs = refs[:pieces], refs[pieces:]
    ups, refs = refs[:pieces], refs[pieces:]
    downs, refs = refs[:pieces], refs[pieces:]
    slope_ref, silu_ref, refs = refs[0], refs[1], refs[2:]
    outs, refs = refs[:peers], refs[peers:]
    gate, up, down, x, gate_grad, up_grad, sems = refs
    copies_d = load_pieces(downs, down, sems.at[2], 1)
    copies_g = load_pieces(gates, gate, sems.at[0], 0)
    copies_u = load_pieces(ups, up, sems.at[1], 0)
    slots = rows[0].shape[0]
    for k, block in enumerate(rows):
        x[k * slots : (k + 1) * slots] = block[...]
    wait_all(copies_d)
    step = 256
    for n in range(gate.shape[1] // step):
        at = slice(n * step, (n + 1) * step)
        hidden_grad = dot_t(x[...], down[at, :])
        gate_grad[:, at] = (hidden_grad * slope_ref[:, at]).astype(BF)
        up_grad[:, at] = (hidden_grad * silu_ref[:, at]).astype(BF)
    wait_all(copies_g)
    wait_all(copies_u)
    step = 512
    for n in range(gate.shape[0] // step):
        at = slice(n * step, (n + 1) * step)
        part = dot_t(gate_grad[...], gate[at, :]) + dot_t(up_grad[...], up[at, :])
        part = part.astype(BF)
        for k, out in enumerate(outs):
            out[:, at] = part[k * slots : (k + 1) * slots]


def mixed(ids_ref, weight_ref, backs, at, cache):
    if not cache:
        first, second, slot = routing(ids_ref, lax.axis_index("expert"))
        slots = backs[0].shape[0]
        for k in range(len(backs)):
            place = placing(slot, k, slots)[:, :slots].astype(BF)
            weight = jnp.where(first == k, weight_ref[0, :, 0:1], 0.0) + jnp.where(
                second == k, weight_ref[0, :, 1:2], 0.0
            )
            cache.append((place, weight))
    total = None
    for back, (place, weight) in zip(backs, cache):
        term = weight * dot(place, back[:, at])
        total = term if total is None else total + term
    return total


def layer_kernel(ids_ref, weight_ref, in_ref, att_ref, *refs):
    backs, out_ref = refs[:-1], refs[-1]
    step, cache = 512, []
    for n in range(in_ref.shape[2] // step):
        at = slice(n * step, (n + 1) * step)
        resid = in_ref[0, :, at].astype(F32) + att_ref[:, at].astype(F32)
        out_ref[0, :, at] = (resid + mixed(ids_ref, weight_ref, backs, at, cache)).astype(BF)


def grad_kernel(ids_ref, weight_ref, in_ref, att_ref, gain_ref, up_ref, *refs):
    backs, out_ref, gained_ref = refs[:-2], refs[-2], refs[-1]
    tok, width = in_ref.shape[1], in_ref.shape[2]
    step, cache = 512, []
    squares = jnp.zeros((tok, 1), F32)
    cross = jnp.zeros((tok, 1), F32)
    for n in range(width // step):
        at = slice(n * step, (n + 1) * step)
        resid = in_ref[0, :, at].astype(F32) + att_ref[:, at].astype(F32)
        gained = gain_ref[:, at] * mixed(ids_ref, weight_ref, backs, at, cache)
        gained_ref[:, at] = gained
        squares = squares + (resid * resid).sum(axis=1, keepdims=True)
        cross = cross + (resid * gained).sum(axis=1, keepdims=True)
    inv_rms = lax.rsqrt(squares / width + 1e-06)
    pull = inv_rms * inv_rms * inv_rms * (cross / width)
    for n in range(width // step):
        at = slice(n * step, (n + 1) * step)
        resid = in_ref[0, :, at].astype(F32) + att_ref[:, at].astype(F32)
        out_ref[0, :, at] = (
            up_ref[0, :, at].astype(F32) + inv_rms * gained_ref[:, at] - resid * pull
        ).astype(BF)


def shards(
    inputs, queries, keys, values, doc_ids, norm_gain, expert_ids, gate_weights, w_gate, w_up, w_down, out_grad
):
    tok, width = inputs.shape[1], inputs.shape[2]
    hidden_count = w_gate.shape[2]
    peers = lax.axis_size("expert")
    slots = 5 * tok // (2 * peers)
    slots = -(-slots // 16) * 16
    pieces = lax.axis_size("fsdp") * lax.axis_size("ctx")
    total = peers * slots
    slab = jax.ShapeDtypeStruct((slots, width), BF)
    slabs = [slab] * peers
    gain = norm_gain.reshape(1, width)

    prev_keys = shifted(keys, ("expert", "ctx"), 1)
    prev_values = shifted(values, ("expert", "ctx"), 1)

    def gathered(weight):
        blocks = []
        for dx in range(lax.axis_size("fsdp")):
            block = weight if dx == 0 else swapped(weight, "fsdp", dx)
            blocks.append(block)
            blocks.append(swapped(block, "ctx", 1))
        return blocks

    gates, ups, downs = gathered(w_gate), gathered(w_up), gathered(w_down)

    def exchanged(blocks):
        return [block if k == 0 else swapped(block, "expert", k) for k, block in enumerate(blocks)]

    sent_grads = pl.pallas_call(
        lambda *refs: pack_kernel(slots, *refs),
        out_shape=slabs,
        in_specs=[VM] * 2,
        out_specs=[VM] * peers,
        compiler_params=params(32),
        name="pack_grad",
    )(expert_ids, out_grad)
    grads = exchanged(sent_grads)

    attended, *sent_rows = pl.pallas_call(
        lambda *refs: attend_kernel(slots, *refs),
        out_shape=[jax.ShapeDtypeStruct((tok, width), BF)] + slabs,
        in_specs=[VM] * 9,
        out_specs=[VM] * (1 + peers),
        compiler_params=params(32),
        name="attend",
    )(queries, keys, values, prev_keys, prev_values, doc_ids, inputs, gain, expert_ids)
    rows = exchanged(sent_rows)

    wide = jax.ShapeDtypeStruct((total, hidden_count), F32)
    weights = [
        pltpu.VMEM((width, hidden_count), BF),
        pltpu.VMEM((width, hidden_count), BF),
        pltpu.VMEM((hidden_count, width), BF),
        pltpu.VMEM((total, width), BF),
    ]
    sems = pltpu.SemaphoreType.DMA((3, pieces))
    *served_out, slope, silu = pl.pallas_call(
        lambda *refs: forward_kernel(peers, pieces, *refs),
        out_shape=slabs + [wide] * 2,
        in_specs=[VM] * peers + [ANY] * (3 * pieces),
        out_specs=[VM] * (peers + 2),
        scratch_shapes=weights + [pltpu.VMEM((total, hidden_count), BF), sems],
        compiler_params=params(48),
        name="forward",
    )(*rows, *gates, *ups, *downs)
    back_out = exchanged(served_out)

    served_grad = pl.pallas_call(
        lambda *refs: backward_kernel(peers, pieces, *refs),
        out_shape=slabs,
        in_specs=[VM] * peers + [ANY] * (3 * pieces) + [VM] * 2,
        out_specs=[VM] * peers,
        scratch_shapes=weights + [pltpu.VMEM((total, hidden_count), BF)] * 2 + [sems],
        compiler_params=params(48),
        name="backward",
    )(*grads, *gates, *ups, *downs, slope, silu)
    back_grad = exchanged(served_grad)

    out_block = jax.ShapeDtypeStruct(inputs.shape, BF)
    layer_out = pl.pallas_call(
        layer_kernel,
        out_shape=out_block,
        in_specs=[VM] * (4 + peers),
        out_specs=VM,
        compiler_params=params(32),
        name="layer",
    )(expert_ids, gate_weights, inputs, attended, *back_out)
    input_grad = pl.pallas_call(
        grad_kernel,
        out_shape=out_block,
        in_specs=[VM] * (6 + peers),
        out_specs=VM,
        scratch_shapes=[pltpu.VMEM((tok, width), F32)],
        compiler_params=params(32),
        name="grad",
    )(expert_ids, gate_weights, inputs, attended, gain, out_grad, *back_grad)
    return layer_out, input_grad


def solution(mesh):
    rows = P(("groups", "fsdp"), ("expert", "ctx"), None)
    in_specs = (
        rows,
        rows,
        rows,
        rows,
        P(("groups", "fsdp"), None),
        P(),
        rows,
        rows,
        P("expert", ("fsdp", "ctx"), None),
        P("expert", ("fsdp", "ctx"), None),
        P("expert", None, ("fsdp", "ctx")),
        rows,
    )
    return jax.shard_map(shards, mesh=mesh, in_specs=in_specs, out_specs=(rows, rows), check_vma=False)
```

```python
import jax
import jax.numpy as jnp
from jax import lax
from jax.experimental import pallas as pl
from jax.experimental.pallas import tpu as pltpu
from jax.sharding import PartitionSpec as P

HEADS = 16
HD = 128
BF = jnp.bfloat16
F32 = jnp.float32
VM = pl.BlockSpec(memory_space=pltpu.VMEM)
ANY = pl.BlockSpec(memory_space=pl.ANY)
MIB = 1024 * 1024


def params(mib):
    return pltpu.CompilerParams(vmem_limit_bytes=mib * MIB)


def swapped(block, axis, distance):
    count = lax.axis_size(axis)
    return lax.ppermute(block, axis, [(i, i ^ distance) for i in range(count)])


def shifted(block, axis, distance):
    devices = range(lax.axis_size(axis))
    route = [(i - distance, i) for i in devices if i - distance in devices]
    return lax.ppermute(block, axis, route)


def after(block, other):
    return lax.optimization_barrier((block, other))[0]


def dot(a, b):
    return jnp.dot(a, b, preferred_element_type=F32)


def dot_t(a, b):
    return lax.dot_general(a, b, (((1,), (1,)), ((), ())), preferred_element_type=F32)


def routing(ids_ref, here):
    tok = ids_ref.shape[1]
    lane = lax.broadcasted_iota(jnp.int32, (tok, 128), 1)
    row = lax.broadcasted_iota(jnp.int32, (tok, tok), 0)
    col = lax.broadcasted_iota(jnp.int32, (tok, tok), 1)
    first, second = ids_ref[0, :, 0:1] ^ here, ids_ref[0, :, 1:2] ^ here
    chosen = (first == lane) | (second == lane)
    before = (col < row).astype(BF)
    rank = dot(before, chosen.astype(BF))
    slot = jnp.where(chosen, rank, -1.0)
    return first, second, slot


def placing(slot, k, slots):
    tok = slot.shape[0]
    lane = lax.broadcasted_iota(jnp.int32, (tok, 128), 1)
    return jnp.where(lane == slot[:, k : k + 1].astype(jnp.int32), 1.0, 0.0)


def pack(rows, slot, slots, out_refs):
    places = [placing(slot, k, slots).T[:slots] for k in range(len(out_refs))]
    table = jnp.concatenate(places, 0).astype(BF)
    packed = dot(table, rows).astype(BF)
    for k, out in enumerate(out_refs):
        out[...] = packed[k * slots : (k + 1) * slots]


def pack_kernel(slots, ids_ref, rows_ref, *out_refs):
    here = lax.axis_index("expert")
    _, _, slot = routing(ids_ref, here)
    pack(rows_ref[0], slot, slots, out_refs)


def attend_kernel(
    slots, q_ref, k_ref, v_ref, kp_ref, vp_ref, doc_ref, in_ref, gain_ref, ids_ref, att_ref, *out_refs
):
    tok = q_ref.shape[1]
    here = lax.axis_index("expert")
    first = (here * lax.axis_size("ctx") + lax.axis_index("ctx")) * tok
    before = jnp.maximum(first - tok, 0)
    own_docs = doc_ref[:, pl.ds(pl.multiple_of(first, tok), tok)]
    past_docs = doc_ref[:, pl.ds(pl.multiple_of(before, tok), tok)]
    row = lax.broadcasted_iota(jnp.int32, (tok, tok), 0)
    col = lax.broadcasted_iota(jnp.int32, (tok, tok), 1)
    own_all = jnp.broadcast_to(own_docs, (tok, tok))
    query_docs = own_all.T
    see_own = (query_docs == own_all) & (col <= row)
    see_past = (query_docs == past_docs) & (first > 0)
    scale = HD ** (-0.5)
    squares = jnp.zeros((tok, HD), F32)
    for h in range(q_ref.shape[2] // HD):
        at = slice(h * HD, (h + 1) * HD)
        q = q_ref[0, :, at]
        own = jnp.where(see_own, dot_t(q, k_ref[0, :, at]) * scale, -jnp.inf)
        past = jnp.where(see_past, dot_t(q, kp_ref[0, :, at]) * scale, -jnp.inf)
        top = jnp.maximum(own, past).max(axis=1, keepdims=True)
        own, past = jnp.exp(own - top), jnp.exp(past - top)
        total = (own + past).sum(axis=1, keepdims=True)
        inverse = 1.0 / total
        own, past = (own * inverse).astype(BF), (past * inverse).astype(BF)
        part = dot(own, v_ref[0, :, at]) + dot(past, vp_ref[0, :, at])
        part = part.astype(BF)
        att_ref[:, at] = part
        resid = in_ref[0, :, at].astype(F32) + part.astype(F32)
        squares = squares + resid * resid
    width = q_ref.shape[2]
    inv_rms = lax.rsqrt(squares.sum(axis=1, keepdims=True) / width + 1e-06)
    resid = in_ref[0].astype(F32) + att_ref[...].astype(F32)
    normed = (resid * inv_rms * gain_ref[...]).astype(BF)
    _, _, slot = routing(ids_ref, here)
    pack(normed, slot, slots, out_refs)


def load_pieces(piece_refs, whole_ref, sems, axis):
    mine = lax.axis_index("fsdp") * lax.axis_size("ctx") + lax.axis_index("ctx")
    size = piece_refs[0].shape[1 + axis]
    copies = []
    for j, piece in enumerate(piece_refs):
        at = pl.ds(pl.multiple_of((mine ^ j) * size, size), size)
        target = whole_ref.at[at, :] if axis == 0 else whole_ref.at[:, at]
        copies.append(pltpu.make_async_copy(piece.at[0], target, sems.at[j]))
    for copy in copies:
        copy.start()
    return copies


def wait_all(copies):
    for copy in copies:
        copy.wait()


def forward_kernel(peers, pieces, *refs):
    rows, refs = refs[:peers], refs[peers:]
    gates, refs = refs[:pieces], refs[pieces:]
    ups, refs = refs[:pieces], refs[pieces:]
    downs, refs = refs[:pieces], refs[pieces:]
    outs, refs = refs[:peers], refs[peers:]
    slope_ref, silu_ref, gate, up, down, x, hidden, sems = refs
    copies_g = load_pieces(gates, gate, sems.at[0], 0)
    copies_u = load_pieces(ups, up, sems.at[1], 0)
    copies_d = load_pieces(downs, down, sems.at[2], 1)
    slots = rows[0].shape[0]
    for k, block in enumerate(rows):
        x[k * slots : (k + 1) * slots] = block[...]
    wait_all(copies_g)
    wait_all(copies_u)
    step = 256
    for n in range(gate.shape[1] // step):
        at = slice(n * step, (n + 1) * step)
        gate_pre = dot(x[...], gate[:, at])
        up_pre = dot(x[...], up[:, at])
        sig = 1.0 / (1.0 + jnp.exp(-gate_pre))
        silu = gate_pre * sig
        hidden[:, at] = (silu * up_pre).astype(BF)
        slope_ref[:, at] = up_pre * sig * (1.0 + gate_pre * (1.0 - sig))
        silu_ref[:, at] = silu
    wait_all(copies_d)
    step = 512
    for n in range(down.shape[1] // step):
        at = slice(n * step, (n + 1) * step)
        part = dot(hidden[...], down[:, at]).astype(BF)
        for k, out in enumerate(outs):
            out[:, at] = part[k * slots : (k + 1) * slots]


def backward_kernel(peers, pieces, *refs):
    rows, refs = refs[:peers], refs[peers:]
    gates, refs = refs[:pieces], refs[pieces:]
    ups, refs = refs[:pieces], refs[pieces:]
    downs, refs = refs[:pieces], refs[pieces:]
    slope_ref, silu_ref, refs = refs[0], refs[1], refs[2:]
    outs, refs = refs[:peers], refs[peers:]
    gate, up, down, x, gate_grad, up_grad, sems = refs
    copies_d = load_pieces(downs, down, sems.at[2], 1)
    copies_g = load_pieces(gates, gate, sems.at[0], 0)
    copies_u = load_pieces(ups, up, sems.at[1], 0)
    slots = rows[0].shape[0]
    for k, block in enumerate(rows):
        x[k * slots : (k + 1) * slots] = block[...]
    wait_all(copies_d)
    step = 256
    for n in range(gate.shape[1] // step):
        at = slice(n * step, (n + 1) * step)
        hidden_grad = dot_t(x[...], down[at, :])
        gate_grad[:, at] = (hidden_grad * slope_ref[:, at]).astype(BF)
        up_grad[:, at] = (hidden_grad * silu_ref[:, at]).astype(BF)
    wait_all(copies_g)
    wait_all(copies_u)
    step = 512
    for n in range(gate.shape[0] // step):
        at = slice(n * step, (n + 1) * step)
        part = dot_t(gate_grad[...], gate[at, :]) + dot_t(up_grad[...], up[at, :])
        part = part.astype(BF)
        for k, out in enumerate(outs):
            out[:, at] = part[k * slots : (k + 1) * slots]


def mixed(ids_ref, weight_ref, backs, at, cache):
    if not cache:
        first, second, slot = routing(ids_ref, lax.axis_index("expert"))
        slots = backs[0].shape[0]
        for k in range(len(backs)):
            place = placing(slot, k, slots)[:, :slots].astype(BF)
            weight = jnp.where(first == k, weight_ref[0, :, 0:1], 0.0) + jnp.where(
                second == k, weight_ref[0, :, 1:2], 0.0
            )
            cache.append((place, weight))
    total = None
    for back, (place, weight) in zip(backs, cache):
        term = weight * dot(place, back[:, at])
        total = term if total is None else total + term
    return total


def layer_kernel(ids_ref, weight_ref, in_ref, att_ref, *refs):
    backs, out_ref = refs[:-1], refs[-1]
    step, cache = 512, []
    for n in range(in_ref.shape[2] // step):
        at = slice(n * step, (n + 1) * step)
        resid = in_ref[0, :, at].astype(F32) + att_ref[:, at].astype(F32)
        out_ref[0, :, at] = (resid + mixed(ids_ref, weight_ref, backs, at, cache)).astype(BF)


def grad_kernel(ids_ref, weight_ref, in_ref, att_ref, gain_ref, up_ref, *refs):
    backs, out_ref, gained_ref = refs[:-2], refs[-2], refs[-1]
    tok, width = in_ref.shape[1], in_ref.shape[2]
    step, cache = 512, []
    squares = jnp.zeros((tok, 1), F32)
    cross = jnp.zeros((tok, 1), F32)
    for n in range(width // step):
        at = slice(n * step, (n + 1) * step)
        resid = in_ref[0, :, at].astype(F32) + att_ref[:, at].astype(F32)
        gained = gain_ref[:, at] * mixed(ids_ref, weight_ref, backs, at, cache)
        gained_ref[:, at] = gained
        squares = squares + (resid * resid).sum(axis=1, keepdims=True)
        cross = cross + (resid * gained).sum(axis=1, keepdims=True)
    inv_rms = lax.rsqrt(squares / width + 1e-06)
    pull = inv_rms * inv_rms * inv_rms * (cross / width)
    for n in range(width // step):
        at = slice(n * step, (n + 1) * step)
        resid = in_ref[0, :, at].astype(F32) + att_ref[:, at].astype(F32)
        out_ref[0, :, at] = (
            up_ref[0, :, at].astype(F32) + inv_rms * gained_ref[:, at] - resid * pull
        ).astype(BF)


def slot_shards(
    inputs, queries, keys, values, doc_ids, norm_gain, expert_ids, gate_weights, w_gate, w_up, w_down, out_grad
):
    tok, width = inputs.shape[1], inputs.shape[2]
    hidden_count = w_gate.shape[2]
    peers = lax.axis_size("expert")
    slots = 5 * tok // (2 * peers)
    slots = -(-slots // 16) * 16
    pieces = lax.axis_size("fsdp") * lax.axis_size("ctx")
    total = peers * slots
    slab = jax.ShapeDtypeStruct((slots, width), BF)
    slabs = [slab] * peers
    gain = norm_gain.reshape(1, width)

    prev_keys = shifted(keys, ("expert", "ctx"), 1)
    prev_values = shifted(values, ("expert", "ctx"), 1)

    def gathered(weight):
        return [weight if dx == 0 else swapped(weight, "fsdp", dx) for dx in range(lax.axis_size("fsdp"))]

    gates, ups, downs = gathered(w_gate), gathered(w_up), gathered(w_down)

    def exchanged(blocks):
        return [block if k == 0 else swapped(block, "expert", k) for k, block in enumerate(blocks)]

    sent_grads = pl.pallas_call(
        lambda *refs: pack_kernel(slots, *refs),
        out_shape=slabs,
        in_specs=[VM] * 2,
        out_specs=[VM] * peers,
        compiler_params=params(32),
        name="pack_grad",
    )(expert_ids, out_grad)
    grads = exchanged(sent_grads)
    queries = after(queries, sent_grads[0])

    attended, *sent_rows = pl.pallas_call(
        lambda *refs: attend_kernel(slots, *refs),
        out_shape=[jax.ShapeDtypeStruct((tok, width), BF)] + slabs,
        in_specs=[VM] * 9,
        out_specs=[VM] * (1 + peers),
        compiler_params=params(32),
        name="attend",
    )(queries, keys, values, prev_keys, prev_values, doc_ids, inputs, gain, expert_ids)
    rows = exchanged(sent_rows)

    def spread(blocks):
        return [part for block in blocks for part in (block, swapped(after(block, attended), "ctx", 1))]

    gates, ups, downs = spread(gates), spread(ups), spread(downs)

    wide = jax.ShapeDtypeStruct((total, hidden_count), F32)
    weights = [
        pltpu.VMEM((width, hidden_count), BF),
        pltpu.VMEM((width, hidden_count), BF),
        pltpu.VMEM((hidden_count, width), BF),
        pltpu.VMEM((total, width), BF),
    ]
    sems = pltpu.SemaphoreType.DMA((3, pieces))
    *served_out, slope, silu = pl.pallas_call(
        lambda *refs: forward_kernel(peers, pieces, *refs),
        out_shape=slabs + [wide] * 2,
        in_specs=[VM] * peers + [ANY] * (3 * pieces),
        out_specs=[VM] * (peers + 2),
        scratch_shapes=weights + [pltpu.VMEM((total, hidden_count), BF), sems],
        compiler_params=params(48),
        name="forward",
    )(*rows, *gates, *ups, *downs)
    back_out = exchanged(served_out)

    served_grad = pl.pallas_call(
        lambda *refs: backward_kernel(peers, pieces, *refs),
        out_shape=slabs,
        in_specs=[VM] * peers + [ANY] * (3 * pieces) + [VM] * 2,
        out_specs=[VM] * peers,
        scratch_shapes=weights + [pltpu.VMEM((total, hidden_count), BF)] * 2 + [sems],
        compiler_params=params(48),
        name="backward",
    )(*grads, *gates, *ups, *downs, slope, silu)
    back_grad = exchanged(served_grad)

    out_block = jax.ShapeDtypeStruct(inputs.shape, BF)
    layer_out = pl.pallas_call(
        layer_kernel,
        out_shape=out_block,
        in_specs=[VM] * (4 + peers),
        out_specs=VM,
        compiler_params=params(32),
        name="layer",
    )(expert_ids, gate_weights, inputs, attended, *back_out)
    input_grad = pl.pallas_call(
        grad_kernel,
        out_shape=out_block,
        in_specs=[VM] * (6 + peers),
        out_specs=VM,
        scratch_shapes=[pltpu.VMEM((tok, width), F32)],
        compiler_params=params(32),
        name="grad",
    )(expert_ids, gate_weights, inputs, attended, gain, out_grad, *back_grad)
    return layer_out, input_grad


def ready(block, *others):
    return lax.optimization_barrier((block, *others))[0]


def lay_kernel(g_ref, u_ref, d_ref, ids_ref, weight_ref, near_ref, far_ref, *refs):
    near, far, router_ref = refs[:3], refs[3:6], refs[6]
    half = g_ref.shape[2] // 2
    unit = half // 3
    group = lax.axis_index("groups")
    for whole, units, start in ((near_ref, near, group), (far_ref, far, 1 - group)):
        at = pl.ds(pl.multiple_of(start * half, half), half)
        for i, block in enumerate((g_ref[0, :, at], u_ref[0, :, at], d_ref[0, at, :].T)):
            whole[i] = block
            for n in range(3):
                units[n][i] = block[:, n * unit : (n + 1) * unit]
    here = lax.axis_index("expert")
    lane = lax.broadcasted_iota(jnp.int32, router_ref.shape, 1)
    first, second = ids_ref[0, :, 0:1] ^ here, ids_ref[0, :, 1:2] ^ here
    router_ref[...] = jnp.where(first == lane, weight_ref[0, :, 0:1], 0.0) + jnp.where(
        second == lane, weight_ref[0, :, 1:2], 0.0
    )


def attend_rows(q_ref, k_ref, v_ref, kp_ref, vp_ref, doc_ref, in_ref, gain_ref, att_ref):
    tok, width = q_ref.shape[1], q_ref.shape[2]
    first = (lax.axis_index("expert") * lax.axis_size("ctx") + lax.axis_index("ctx")) * tok
    before = jnp.maximum(first - tok, 0)
    own_docs = doc_ref[:, pl.ds(pl.multiple_of(first, tok), tok)]
    past_docs = doc_ref[:, pl.ds(pl.multiple_of(before, tok), tok)]
    row = lax.broadcasted_iota(jnp.int32, (tok, tok), 0)
    col = lax.broadcasted_iota(jnp.int32, (tok, tok), 1)
    own_all = jnp.broadcast_to(own_docs, (tok, tok))
    query_docs = own_all.T
    see_own = (query_docs == own_all) & (col <= row)
    see_past = (query_docs == past_docs) & (first > 0)
    scale = HD ** (-0.5)
    squares = jnp.zeros((tok, HD), F32)
    for h in range(width // HD):
        at = slice(h * HD, (h + 1) * HD)
        q = q_ref[0, :, at]
        own = jnp.where(see_own, dot_t(q, k_ref[0, :, at]) * scale, -jnp.inf)
        past = jnp.where(see_past, dot_t(q, kp_ref[0, :, at]) * scale, -jnp.inf)
        top = jnp.maximum(own, past).max(axis=1, keepdims=True)
        own, past = jnp.exp(own - top), jnp.exp(past - top)
        total = (own + past).sum(axis=1, keepdims=True)
        inverse = 1.0 / total
        own, past = (own * inverse).astype(BF), (past * inverse).astype(BF)
        part = dot(own, v_ref[0, :, at]) + dot(past, vp_ref[0, :, at])
        part = part.astype(BF)
        att_ref[:, at] = part
        resid = in_ref[0, :, at].astype(F32) + part.astype(F32)
        squares = squares + resid * resid
    inv_rms = lax.rsqrt(squares.sum(axis=1, keepdims=True) / width + 1e-06)
    resid = in_ref[0].astype(F32) + att_ref[...].astype(F32)
    return (resid * inv_rms * gain_ref[...]).astype(BF)


def normed_kernel(*refs):
    refs[-1][...] = attend_rows(*refs[:-1])


def load_units(groups, piece_refs, whole_ref, sems):
    mine = lax.axis_index("fsdp") * lax.axis_size("ctx") + lax.axis_index("ctx")
    copies, start = [], 0
    for g, (_, count) in enumerate(groups):
        for j in range(4):
            piece = piece_refs[4 * g + j]
            size = piece.shape[1]
            at = pl.ds(pl.multiple_of((mine ^ j) * size, size), size)
            target = whole_ref.at[:, at, start : start + count]
            copies.append(pltpu.make_async_copy(piece, target, sems.at[4 * g + j]))
        start += count
    for copy in copies:
        copy.start()
    return copies


def spans(groups):
    found, start = [], 0
    for expert, count in groups:
        if found and found[-1][0] == expert and found[-1][2] - found[-1][1] + count <= 256:
            found[-1][2] = start + count
        else:
            found.append([expert, start, start + count])
        start += count
    return found


def join(x, own_ref, pair_ref):
    tok = x.shape[0] // 2
    own, pair = own_ref, pair_ref
    x[:tok] = own[...].reshape(tok, x.shape[1])
    x[tok:] = pair[...].reshape(tok, x.shape[1])


def router_columns(router_ref, pair_router_ref):
    return [
        jnp.concatenate([router_ref[:, 2 * e : 2 * e + 1], pair_router_ref[:, 2 * e + 1 : 2 * e + 2]], 0)
        for e in range(2)
    ]


def slice_grads(groups, whole, x, y, hidden, gate_grad, up_grad):
    for _, lo, hi in spans(groups):
        gate_pre = dot(x[...], whole[0, :, lo:hi])
        up_pre = dot(x[...], whole[1, :, lo:hi])
        hidden_grad = dot(y[...], whole[2, :, lo:hi])
        sig = 1.0 / (1.0 + jnp.exp(-gate_pre))
        silu = gate_pre * sig
        hidden[:, lo:hi] = (silu * up_pre).astype(BF)
        gate_grad[:, lo:hi] = (hidden_grad * up_pre * sig * (1.0 + gate_pre * (1.0 - sig))).astype(BF)
        up_grad[:, lo:hi] = (hidden_grad * silu).astype(BF)


def experts_of(groups):
    found, start = [], 0
    for expert, count in groups:
        if found and found[-1][0] == expert:
            found[-1][2] = start + count
        else:
            found.append([expert, start, start + count])
        start += count
    return found


def slice_kernel(groups, carried, *refs):
    rows, pair_rows, grads, pair_grads, router_ref, pair_router_ref = refs[:6]
    refs = refs[6:]
    pieces, refs = refs[: 4 * len(groups)], refs[4 * len(groups) :]
    if carried:
        out_in, grad_in, refs = refs[0], refs[1], refs[2:]
    out_sum, grad_sum, whole, x, y, hidden, gate_grad, up_grad, sems = refs
    copies = load_units(groups, pieces, whole, sems)
    join(x, rows, pair_rows)
    join(y, grads, pair_grads)
    weights = router_columns(router_ref, pair_router_ref)
    for copy in copies:
        copy.wait()
    slice_grads(groups, whole, x, y, hidden, gate_grad, up_grad)
    step = 512
    for n in range(x.shape[1] // step):
        at = slice(n * step, (n + 1) * step)
        out_term = out_in[:, at] if carried else None
        grad_term = grad_in[:, at] if carried else None
        for expert, lo, hi in experts_of(groups):
            w = weights[expert]
            out_new = w * dot_t(hidden[:, lo:hi], whole[2, at, lo:hi])
            grad_new = w * (
                dot_t(gate_grad[:, lo:hi], whole[0, at, lo:hi]) + dot_t(up_grad[:, lo:hi], whole[1, at, lo:hi])
            )
            out_term = out_new if out_term is None else out_term + out_new
            grad_term = grad_new if grad_term is None else grad_term + grad_new
        out_sum[:, at] = out_term
        grad_sum[:, at] = grad_term


def last_out_kernel(groups, *refs):
    rows, pair_rows, grads, pair_grads, router_ref, pair_router_ref = refs[:6]
    refs = refs[6:]
    pieces, refs = refs[: 4 * len(groups)], refs[4 * len(groups) :]
    out_in, own_out, pair_out, gate_grad, up_grad, whole, x, y, hidden, sems = refs
    copies = load_units(groups, pieces, whole, sems)
    join(x, rows, pair_rows)
    join(y, grads, pair_grads)
    weights = router_columns(router_ref, pair_router_ref)
    for copy in copies:
        copy.wait()
    slice_grads(groups, whole, x, y, hidden, gate_grad, up_grad)
    tok, step = own_out.shape[0], 512
    for n in range(x.shape[1] // step):
        at = slice(n * step, (n + 1) * step)
        total = out_in[:, at]
        for expert, lo, hi in experts_of(groups):
            total = total + weights[expert] * dot_t(hidden[:, lo:hi], whole[2, at, lo:hi])
        own_out[:, at] = total[:tok]
        pair_out[:, at] = total[tok:].astype(BF)


def last_grad_kernel(groups, router_ref, pair_router_ref, *refs):
    pieces, refs = refs[: 4 * len(groups)], refs[4 * len(groups) :]
    gate_grad, up_grad, grad_in, own_grad, pair_grad, whole, sems = refs
    copies = load_units(groups, pieces, whole, sems)
    weights = router_columns(router_ref, pair_router_ref)
    for copy in copies:
        copy.wait()
    tok, step = own_grad.shape[0], 512
    for n in range(grad_in.shape[1] // step):
        at = slice(n * step, (n + 1) * step)
        total = grad_in[:, at]
        for expert, lo, hi in experts_of(groups):
            total = total + weights[expert] * (
                dot_t(gate_grad[:, lo:hi], whole[0, at, lo:hi]) + dot_t(up_grad[:, lo:hi], whole[1, at, lo:hi])
            )
        own_grad[:, at] = total[:tok]
        pair_grad[:, at] = total[tok:].astype(BF)


def pair_layer_kernel(in_ref, att_ref, own_ref, back_ref, out_ref):
    resid = in_ref[0].astype(F32) + att_ref[...].astype(F32)
    out_ref[0] = (resid + own_ref[...] + back_ref[...].astype(F32)).astype(BF)


def pair_grad_kernel(in_ref, att_ref, gain_ref, up_ref, own_ref, back_ref, out_ref):
    width = in_ref.shape[2]
    resid = in_ref[0].astype(F32) + att_ref[...].astype(F32)
    gained = gain_ref[...] * (own_ref[...] + back_ref[...].astype(F32))
    inv_rms = lax.rsqrt((resid * resid).sum(axis=1, keepdims=True) / width + 1e-06)
    pull = inv_rms * inv_rms * inv_rms * ((resid * gained).sum(axis=1, keepdims=True) / width)
    out_ref[0] = (up_ref[0].astype(F32) + inv_rms * gained - resid * pull).astype(BF)


def pair_shards(
    inputs, queries, keys, values, doc_ids, norm_gain, expert_ids, gate_weights, w_gate, w_up, w_down, out_grad
):
    tok, width = inputs.shape[1], inputs.shape[2]
    half = w_gate.shape[2] // 2
    unit = half // 3
    shard = w_gate.shape[1]
    gain = norm_gain.reshape(1, width)

    def shape(*dims, kind=BF):
        return jax.ShapeDtypeStruct(dims, kind)

    def call(kernel, name, out_shape, in_specs, scratch=(), mib=32, aliases=None):
        single = not isinstance(out_shape, list)
        return pl.pallas_call(
            kernel,
            out_shape=out_shape,
            in_specs=in_specs,
            out_specs=VM if single else [VM] * len(out_shape),
            scratch_shapes=list(scratch),
            input_output_aliases=aliases or {},
            compiler_params=params(mib),
            name=name,
        )

    def over_x(block):
        return swapped(block, "fsdp", 1)

    def over_y(block):
        return swapped(block, "groups", 1)

    def over_core(block):
        return swapped(block, "ctx", 1)

    prev_keys = shifted(keys, ("expert", "ctx"), 1)
    prev_values = shifted(values, ("expert", "ctx"), 1)

    big, small = shape(3, shard, half), shape(3, shard, unit)
    near, far, *laid = call(lay_kernel, "lay", [big, big] + [small] * 6 + [shape(tok, 128, kind=F32)], [VM] * 5)(
        w_gate, w_up, w_down, expert_ids, gate_weights
    )
    near_units, far_units, router = laid[:3], laid[3:6], laid[6]
    own_near_x = over_x(near)
    z_units = [swapped(near_units[0], "expert", 2), swapped(near_units[1], "expert", 2)]
    pair_router = swapped(router, "expert", 1)
    pair_grads = swapped(out_grad, "expert", 1)
    near_core, far_core = over_core(near), over_core(far)

    attended, rows = call(
        lambda *refs: normed_kernel(*refs), "attend", [shape(tok, width)] * 2, [VM] * 8
    )(queries, keys, values, prev_keys, prev_values, doc_ids, inputs, gain)
    pair_rows = swapped(rows, "expert", 1)

    def both(block):
        return [block, over_core(block)]

    def spread_near(block):
        return over_x(block), over_y(block)

    zero = ready(z_units[0], rows)
    z_units.append(swapped(ready(near_units[2], zero), "expert", 2))
    x0, y0 = spread_near(zero)
    own_near = [near, near_core] + both(ready(own_near_x, rows))
    far_x = [over_x(ready(far_units[0], zero))]

    scratch = lambda count: [
        pltpu.VMEM((3, width, count), BF),
        pltpu.VMEM((2 * tok, width), BF),
        pltpu.VMEM((2 * tok, width), BF),
    ]
    acts = lambda count, number: [pltpu.VMEM((2 * tok, count), BF)] * number
    sems = lambda groups: [pltpu.SemaphoreType.DMA((4 * len(groups),))]
    sums = [shape(2 * tok, width, kind=F32)] * 2
    token_args = [rows, pair_rows, out_grad, pair_grads, router, pair_router]

    groups = ((0, half),)
    out_sum, grad_sum = call(
        lambda *refs: slice_kernel(((0, half),), False, *refs),
        "slice_a",
        sums,
        [VM] * 6 + [ANY] * 4,
        scratch(half) + acts(half, 3) + sems(groups),
        48,
    )(*token_args[:1], *token_args[1:], *own_near)

    xy0 = over_y(ready(x0, out_sum))
    unit_pieces = lambda z, x, y, xy: (both(z) + both(x), both(y) + both(xy))
    one = ready(z_units[1], out_sum)
    x1, y1 = spread_near(one)
    far_x.append(over_x(ready(far_units[1], one)))
    two = z_units[2]
    xy1 = over_y(x1)
    x2, y2 = spread_near(ready(two, one))
    far_x.append(over_x(ready(far_units[2], two)))
    near0, away0 = unit_pieces(zero, x0, y0, xy0)
    near1, away1 = unit_pieces(one, x1, y1, xy1)

    def home(i):
        return [far_units[i], over_core(far_units[i])] + both(far_x[i])

    mid_groups = ((1, unit),) * 4 + ((0, unit),) * 2
    mid_pieces = near0 + away0 + near1 + away1 + home(0) + home(1)
    count = 6 * unit
    out_sum, grad_sum = call(
        lambda *refs: slice_kernel(mid_groups, True, *refs),
        "slice_b",
        sums,
        [VM] * 6 + [ANY] * 24 + [VM] * 2,
        scratch(count) + acts(count, 3) + sems(mid_groups),
        56,
        {30: 0, 31: 1},
    )(*token_args, *mid_pieces, out_sum, grad_sum)

    xy2 = over_y(x2)
    near2, away2 = unit_pieces(two, x2, y2, xy2)
    last_groups = ((1, unit),) * 2 + ((0, unit),)
    last_pieces = near2 + away2 + home(2)
    count = 3 * unit
    act = shape(2 * tok, count)
    own_out, pair_out, gate_grad, up_grad = call(
        lambda *refs: last_out_kernel(last_groups, *refs),
        "slice_out",
        [shape(tok, width, kind=F32), shape(tok, width), act, act],
        [VM] * 6 + [ANY] * 12 + [VM],
        scratch(count) + acts(count, 1) + sems(last_groups),
        48,
    )(*token_args, *last_pieces, out_sum)
    back_out = swapped(pair_out, "expert", 1)
    own_grad, pair_grad = call(
        lambda *refs: last_grad_kernel(last_groups, *refs),
        "slice_grad",
        [shape(tok, width, kind=F32), shape(tok, width)],
        [VM] * 2 + [ANY] * 12 + [VM] * 3,
        scratch(count)[:1] + sems(last_groups),
        48,
    )(router, pair_router, *last_pieces, gate_grad, up_grad, grad_sum)
    back_grad = swapped(pair_grad, "expert", 1)

    block = jax.ShapeDtypeStruct(inputs.shape, BF)
    layer_out = call(pair_layer_kernel, "layer", block, [VM] * 4)(inputs, attended, own_out, back_out)
    input_grad = call(pair_grad_kernel, "grad", block, [VM] * 6)(
        inputs, attended, gain, out_grad, own_grad, back_grad
    )
    return layer_out, input_grad


def solution(mesh):
    rows = P(("groups", "fsdp"), ("expert", "ctx"), None)
    in_specs = (
        rows,
        rows,
        rows,
        rows,
        P(("groups", "fsdp"), None),
        P(),
        rows,
        rows,
        P("expert", ("fsdp", "ctx"), None),
        P("expert", ("fsdp", "ctx"), None),
        P("expert", None, ("fsdp", "ctx")),
        rows,
    )
    paired = (mesh.shape["expert"], mesh.shape["fsdp"], mesh.shape["groups"], mesh.shape["ctx"]) == (4, 2, 2, 2)
    shards = pair_shards if paired else slot_shards
    return jax.shard_map(shards, mesh=mesh, in_specs=in_specs, out_specs=(rows, rows), check_vma=False)
```

```python
import jax
import jax.numpy as jnp
from jax import lax
from jax.experimental import pallas as pl
from jax.experimental.pallas import tpu as pltpu
from jax.sharding import PartitionSpec as P

HEADS = 16
HD = 128
BF = jnp.bfloat16
F32 = jnp.float32
VM = pl.BlockSpec(memory_space=pltpu.VMEM)
ANY = pl.BlockSpec(memory_space=pl.ANY)
MIB = 1024 * 1024


def params(mib):
    return pltpu.CompilerParams(vmem_limit_bytes=mib * MIB)


def swapped(block, axis, distance):
    count = lax.axis_size(axis)
    return lax.ppermute(block, axis, [(i, i ^ distance) for i in range(count)])


def shifted(block, axis, distance):
    devices = range(lax.axis_size(axis))
    route = [(i - distance, i) for i in devices if i - distance in devices]
    return lax.ppermute(block, axis, route)


def after(block, *others):
    return lax.optimization_barrier((block, *others))[0]


def dot(a, b):
    return jnp.dot(a, b, preferred_element_type=F32)


def dot_t(a, b):
    return lax.dot_general(a, b, (((1,), (1,)), ((), ())), preferred_element_type=F32)


def column(row):
    tok = row.shape[1]
    return jnp.broadcast_to(row, (tok, tok)).T[:, 0:1]


def routing(ids_ref, here):
    tok = ids_ref.shape[2]
    lane = lax.broadcasted_iota(jnp.int32, (tok, 128), 1)
    row = lax.broadcasted_iota(jnp.int32, (tok, tok), 0)
    col = lax.broadcasted_iota(jnp.int32, (tok, tok), 1)
    first, second = column(ids_ref[0, 0:1]) ^ here, column(ids_ref[0, 1:2]) ^ here
    chosen = (first == lane) | (second == lane)
    before = (col < row).astype(BF)
    rank = dot(before, chosen.astype(BF))
    slot = jnp.where(chosen, rank, -1.0)
    return first, second, slot


def placing(slot, k, slots):
    tok = slot.shape[0]
    lane = lax.broadcasted_iota(jnp.int32, (tok, 128), 1)
    return jnp.where(lane == slot[:, k : k + 1].astype(jnp.int32), 1.0, 0.0)


def pack(rows, slot, slots, out_refs):
    places = [placing(slot, k, slots).T[:slots] for k in range(len(out_refs))]
    table = jnp.concatenate(places, 0).astype(BF)
    packed = dot(table, rows).astype(BF)
    for k, out in enumerate(out_refs):
        out[...] = packed[k * slots : (k + 1) * slots]


def prepare_kernel(slots, ids_ref, rows_hbm, g_hbm, u_hbm, d_hbm, weight_ref, *refs):
    out_refs, (rows, down, sems) = refs[:-3], refs[-3:]
    copies = [
        pltpu.make_async_copy(rows_hbm.at[0], rows, sems.at[0]),
        pltpu.make_async_copy(d_hbm.at[0], down, sems.at[1]),
        pltpu.make_async_copy(g_hbm.at[0], weight_ref.at[0], sems.at[2]),
        pltpu.make_async_copy(u_hbm.at[0], weight_ref.at[1], sems.at[3]),
    ]
    for copy in copies:
        copy.start()
    _, _, slot = routing(ids_ref, lax.axis_index("expert"))
    copies[0].wait()
    pack(rows[...], slot, slots, out_refs)
    copies[1].wait()
    weight_ref[2] = down[...].T
    copies[2].wait()
    copies[3].wait()


def attend_kernel(
    slots, q_ref, k_ref, v_ref, kp_ref, vp_ref, doc_ref, in_ref, gain_ref, ids_ref, att_ref, *out_refs
):
    tok = q_ref.shape[1]
    here = lax.axis_index("expert")
    first = (here * lax.axis_size("ctx") + lax.axis_index("ctx")) * tok
    before = jnp.maximum(first - tok, 0)
    own_docs = doc_ref[:, pl.ds(pl.multiple_of(first, tok), tok)]
    past_docs = doc_ref[:, pl.ds(pl.multiple_of(before, tok), tok)]
    row = lax.broadcasted_iota(jnp.int32, (tok, tok), 0)
    col = lax.broadcasted_iota(jnp.int32, (tok, tok), 1)
    own_all = jnp.broadcast_to(own_docs, (tok, tok))
    query_docs = own_all.T
    see_own = (query_docs == own_all) & (col <= row)
    see_past = (query_docs == past_docs) & (first > 0)
    scale = HD ** (-0.5)
    squares = jnp.zeros((tok, HD), F32)
    for h in range(q_ref.shape[2] // HD):
        at = slice(h * HD, (h + 1) * HD)
        q = q_ref[0, :, at]
        own = jnp.where(see_own, dot_t(q, k_ref[0, :, at]) * scale, -jnp.inf)
        past = jnp.where(see_past, dot_t(q, kp_ref[0, :, at]) * scale, -jnp.inf)
        top = jnp.maximum(own, past).max(axis=1, keepdims=True)
        own, past = jnp.exp(own - top), jnp.exp(past - top)
        total = (own + past).sum(axis=1, keepdims=True)
        inverse = 1.0 / total
        own, past = (own * inverse).astype(BF), (past * inverse).astype(BF)
        part = dot(own, v_ref[0, :, at]) + dot(past, vp_ref[0, :, at])
        part = part.astype(BF)
        att_ref[:, at] = part
        resid = in_ref[0, :, at].astype(F32) + part.astype(F32)
        squares = squares + resid * resid
    width = q_ref.shape[2]
    inv_rms = lax.rsqrt(squares.sum(axis=1, keepdims=True) / width + 1e-06)
    resid = in_ref[0].astype(F32) + att_ref[...].astype(F32)
    normed = (resid * inv_rms * gain_ref[...]).astype(BF)
    _, _, slot = routing(ids_ref, here)
    pack(normed, slot, slots, out_refs)


def load_pieces(piece_refs, whole_ref, sems):
    mine = lax.axis_index("fsdp") * lax.axis_size("ctx") + lax.axis_index("ctx")
    size = piece_refs[0].shape[1]
    copies = []
    for j, piece in enumerate(piece_refs):
        at = pl.ds(pl.multiple_of((mine ^ j) * size, size), size)
        copies.append(pltpu.make_async_copy(piece, whole_ref.at[:, at], sems.at[j]))
    for copy in copies:
        copy.start()
    return copies


def forward_kernel(peers, pieces, *refs):
    rows, refs = refs[:peers], refs[peers:]
    weights, refs = refs[:pieces], refs[pieces:]
    outs, refs = refs[:peers], refs[peers:]
    slope_ref, silu_ref, whole, x, hidden, sems = refs
    copies = load_pieces(weights, whole, sems)
    slots = rows[0].shape[0]
    for k, block in enumerate(rows):
        x[k * slots : (k + 1) * slots] = block[...]
    for copy in copies:
        copy.wait()
    step = 256
    for n in range(whole.shape[2] // step):
        at = slice(n * step, (n + 1) * step)
        gate_pre = dot(x[...], whole[0, :, at])
        up_pre = dot(x[...], whole[1, :, at])
        sig = 1.0 / (1.0 + jnp.exp(-gate_pre))
        silu = gate_pre * sig
        hidden[:, at] = (silu * up_pre).astype(BF)
        slope_ref[:, at] = up_pre * sig * (1.0 + gate_pre * (1.0 - sig))
        silu_ref[:, at] = silu
    step = 512
    for n in range(whole.shape[1] // step):
        at = slice(n * step, (n + 1) * step)
        part = dot_t(hidden[...], whole[2, at]).astype(BF)
        for k, out in enumerate(outs):
            out[:, at] = part[k * slots : (k + 1) * slots]


def backward_kernel(peers, pieces, *refs):
    rows, refs = refs[:peers], refs[peers:]
    weights, refs = refs[:pieces], refs[pieces:]
    slope_ref, silu_ref, refs = refs[0], refs[1], refs[2:]
    outs, refs = refs[:peers], refs[peers:]
    whole, x, gate_grad, up_grad, sems = refs
    copies = load_pieces(weights, whole, sems)
    slots = rows[0].shape[0]
    for k, block in enumerate(rows):
        x[k * slots : (k + 1) * slots] = block[...]
    for copy in copies:
        copy.wait()
    step = 256
    for n in range(whole.shape[2] // step):
        at = slice(n * step, (n + 1) * step)
        hidden_grad = dot(x[...], whole[2, :, at])
        gate_grad[:, at] = (hidden_grad * slope_ref[:, at]).astype(BF)
        up_grad[:, at] = (hidden_grad * silu_ref[:, at]).astype(BF)
    step = 512
    for n in range(whole.shape[1] // step):
        at = slice(n * step, (n + 1) * step)
        part = dot_t(gate_grad[...], whole[0, at]) + dot_t(up_grad[...], whole[1, at])
        part = part.astype(BF)
        for k, out in enumerate(outs):
            out[:, at] = part[k * slots : (k + 1) * slots]


def mixed(ids_ref, weight_ref, backs, at, cache):
    if not cache:
        first, second, slot = routing(ids_ref, lax.axis_index("expert"))
        slots = backs[0].shape[0]
        gates = [column(weight_ref[0, j : j + 1]) for j in range(2)]
        for k in range(len(backs)):
            place = placing(slot, k, slots)[:, :slots].astype(BF)
            weight = jnp.where(first == k, gates[0], 0.0) + jnp.where(second == k, gates[1], 0.0)
            cache.append((place, weight))
    total = None
    for back, (place, weight) in zip(backs, cache):
        term = weight * dot(place, back[:, at])
        total = term if total is None else total + term
    return total


def layer_kernel(ids_ref, weight_ref, in_ref, att_ref, *refs):
    backs, out_ref = refs[:-1], refs[-1]
    step, cache = 512, []
    for n in range(in_ref.shape[2] // step):
        at = slice(n * step, (n + 1) * step)
        resid = in_ref[0, :, at].astype(F32) + att_ref[:, at].astype(F32)
        out_ref[0, :, at] = (resid + mixed(ids_ref, weight_ref, backs, at, cache)).astype(BF)


def grad_kernel(ids_ref, weight_ref, in_ref, att_ref, gain_ref, up_ref, *refs):
    backs, out_ref, gained_ref = refs[:-2], refs[-2], refs[-1]
    tok, width = in_ref.shape[1], in_ref.shape[2]
    step, cache = 512, []
    squares = jnp.zeros((tok, 1), F32)
    cross = jnp.zeros((tok, 1), F32)
    for n in range(width // step):
        at = slice(n * step, (n + 1) * step)
        resid = in_ref[0, :, at].astype(F32) + att_ref[:, at].astype(F32)
        gained = gain_ref[:, at] * mixed(ids_ref, weight_ref, backs, at, cache)
        gained_ref[:, at] = gained
        squares = squares + (resid * resid).sum(axis=1, keepdims=True)
        cross = cross + (resid * gained).sum(axis=1, keepdims=True)
    inv_rms = lax.rsqrt(squares / width + 1e-06)
    pull = inv_rms * inv_rms * inv_rms * (cross / width)
    for n in range(width // step):
        at = slice(n * step, (n + 1) * step)
        resid = in_ref[0, :, at].astype(F32) + att_ref[:, at].astype(F32)
        out_ref[0, :, at] = (
            up_ref[0, :, at].astype(F32) + inv_rms * gained_ref[:, at] - resid * pull
        ).astype(BF)


def shards(
    inputs, queries, keys, values, doc_ids, norm_gain, expert_ids, gate_weights, w_gate, w_up, w_down, out_grad
):
    tok, width = inputs.shape[1], inputs.shape[2]
    hidden_count = w_gate.shape[2]
    peers = lax.axis_size("expert")
    slots = 5 * tok // (2 * peers)
    slots = -(-slots // 16) * 16
    pieces = lax.axis_size("fsdp") * lax.axis_size("ctx")
    total = peers * slots
    slab = jax.ShapeDtypeStruct((slots, width), BF)
    slabs = [slab] * peers
    gain = norm_gain.reshape(1, width)
    ids, gates = jnp.swapaxes(expert_ids, 1, 2), jnp.swapaxes(gate_weights, 1, 2)

    prev_keys = shifted(keys, ("expert", "ctx"), 1)
    prev_values = shifted(values, ("expert", "ctx"), 1)

    def exchanged(blocks):
        return [block if k == 0 else swapped(block, "expert", k) for k, block in enumerate(blocks)]

    own_weights, *sent_grads = pl.pallas_call(
        lambda *refs: prepare_kernel(slots, *refs),
        out_shape=[jax.ShapeDtypeStruct((3, w_gate.shape[1], hidden_count), BF)] + slabs,
        in_specs=[VM] + [ANY] * 4,
        out_specs=[VM] * (1 + peers),
        scratch_shapes=[
            pltpu.VMEM((tok, width), BF),
            pltpu.VMEM(w_down.shape[1:], BF),
            pltpu.SemaphoreType.DMA((4,)),
        ],
        compiler_params=params(32),
        name="prepare",
    )(ids, out_grad, w_gate, w_up, w_down)
    early = exchanged(sent_grads[:-1])
    weights = [own_weights] + [swapped(own_weights, "fsdp", dx) for dx in range(1, lax.axis_size("fsdp"))]

    attended, *sent_rows = pl.pallas_call(
        lambda *refs: attend_kernel(slots, *refs),
        out_shape=[jax.ShapeDtypeStruct((tok, width), BF)] + slabs,
        in_specs=[VM] * 9,
        out_specs=[VM] * (1 + peers),
        compiler_params=params(32),
        name="attend",
    )(after(queries, own_weights), keys, values, prev_keys, prev_values, doc_ids, inputs, gain, ids)
    grads = early + [swapped(after(sent_grads[-1], attended), "expert", peers - 1)]
    rows = exchanged([after(block, early[-1]) for block in sent_rows])
    weights = [part for block in weights for part in (block, swapped(after(block, rows[-2], *early[1:]), "ctx", 1))]

    wide = jax.ShapeDtypeStruct((total, hidden_count), F32)
    scratch = [pltpu.VMEM((3, width, hidden_count), BF), pltpu.VMEM((total, width), BF)]
    sems = pltpu.SemaphoreType.DMA((pieces,))
    *served_out, slope, silu = pl.pallas_call(
        lambda *refs: forward_kernel(peers, pieces, *refs),
        out_shape=slabs + [wide] * 2,
        in_specs=[VM] * peers + [ANY] * pieces,
        out_specs=[VM] * (peers + 2),
        scratch_shapes=scratch + [pltpu.VMEM((total, hidden_count), BF), sems],
        compiler_params=params(48),
        name="forward",
    )(*rows, *weights)
    back_out = exchanged(served_out)

    served_grad = pl.pallas_call(
        lambda *refs: backward_kernel(peers, pieces, *refs),
        out_shape=slabs,
        in_specs=[VM] * peers + [ANY] * pieces + [VM] * 2,
        out_specs=[VM] * peers,
        scratch_shapes=scratch + [pltpu.VMEM((total, hidden_count), BF)] * 2 + [sems],
        compiler_params=params(48),
        name="backward",
    )(*grads, *weights, slope, silu)
    back_grad = exchanged(served_grad)

    out_block = jax.ShapeDtypeStruct(inputs.shape, BF)
    layer_out = pl.pallas_call(
        layer_kernel,
        out_shape=out_block,
        in_specs=[VM] * (4 + peers),
        out_specs=VM,
        compiler_params=params(32),
        name="layer",
    )(ids, gates, inputs, attended, *back_out)
    input_grad = pl.pallas_call(
        grad_kernel,
        out_shape=out_block,
        in_specs=[VM] * (6 + peers),
        out_specs=VM,
        scratch_shapes=[pltpu.VMEM((tok, width), F32)],
        compiler_params=params(32),
        name="grad",
    )(ids, gates, inputs, after(attended, layer_out), gain, out_grad, *back_grad)
    return layer_out, input_grad


def solution(mesh):
    rows = P(("groups", "fsdp"), ("expert", "ctx"), None)
    in_specs = (
        rows,
        rows,
        rows,
        rows,
        P(("groups", "fsdp"), None),
        P(),
        rows,
        rows,
        P("expert", ("fsdp", "ctx"), None),
        P("expert", ("fsdp", "ctx"), None),
        P("expert", None, ("fsdp", "ctx")),
        rows,
    )
    return jax.shard_map(shards, mesh=mesh, in_specs=in_specs, out_specs=(rows, rows), check_vma=False)
```

```python
import jax
import jax.numpy as jnp
from jax import lax
from jax.experimental import pallas as pl
from jax.experimental.pallas import tpu as pltpu
from jax.sharding import PartitionSpec as P

HEADS = 16
HD = 128
BF = jnp.bfloat16
F32 = jnp.float32
VM = pl.BlockSpec(memory_space=pltpu.VMEM)
MIB = 1024 * 1024


def params(mib):
    return pltpu.CompilerParams(vmem_limit_bytes=mib * MIB)


def swapped(block, axis, distance):
    count = lax.axis_size(axis)
    return lax.ppermute(block, axis, [(i, i ^ distance) for i in range(count)])


def shifted(block, axis, distance):
    devices = range(lax.axis_size(axis))
    route = [(i - distance, i) for i in devices if i - distance in devices]
    return lax.ppermute(block, axis, route)


def after(block, *others):
    return lax.optimization_barrier((block, *others))[0]


def dot(a, b):
    return jnp.dot(a, b, preferred_element_type=F32)


def dot_t(a, b):
    return lax.dot_general(a, b, (((1,), (1,)), ((), ())), preferred_element_type=F32)


def column(row):
    tok = row.shape[1]
    return jnp.broadcast_to(row, (tok, tok)).T[:, 0:1]


def routing(first, second, here):
    tok = first.shape[1]
    lane = lax.broadcasted_iota(jnp.int32, (tok, 128), 1)
    row = lax.broadcasted_iota(jnp.int32, (tok, tok), 0)
    col = lax.broadcasted_iota(jnp.int32, (tok, tok), 1)
    first, second = column(first) ^ here, column(second) ^ here
    chosen = (first == lane) | (second == lane)
    before = (col < row).astype(BF)
    rank = dot(before, chosen.astype(BF))
    slot = jnp.where(chosen, rank, -1.0)
    return first, second, slot


def placing(slot, k, slots):
    tok = slot.shape[0]
    lane = lax.broadcasted_iota(jnp.int32, (tok, 128), 1)
    return jnp.where(lane == slot[:, k : k + 1].astype(jnp.int32), 1.0, 0.0)


def placing_table(slot, slots, count):
    return jnp.concatenate([placing(slot, k, slots).T[:slots] for k in range(count)], 0).astype(BF)


def pack(rows, slot, slots, out_refs):
    packed = dot(placing_table(slot, slots, len(out_refs)), rows).astype(BF)
    for k, out in enumerate(out_refs):
        out[...] = packed[k * slots : (k + 1) * slots]


def prepare_kernel(slots, ids_ref, k_hbm, v_hbm, rows_hbm, g_hbm, u_hbm, d_hbm, both_hbm, weight_hbm, *refs):
    out_refs, (both, weight, rows, down, sems) = refs[:-5], refs[-5:]
    pairs = [
        (k_hbm.at[0], both.at[0]),
        (v_hbm.at[0], both.at[1]),
        (d_hbm.at[0], down),
        (g_hbm.at[0], weight.at[0]),
        (u_hbm.at[0], weight.at[1]),
        (rows_hbm.at[0], rows),
        (both.at[0], both_hbm.at[0]),
        (both.at[1], both_hbm.at[1]),
        (weight.at[0], weight_hbm.at[0]),
        (weight.at[1], weight_hbm.at[1]),
        (weight.at[2], weight_hbm.at[2]),
    ]
    copies = [pltpu.make_async_copy(source, target, sems.at[n]) for n, (source, target) in enumerate(pairs)]
    for copy in copies[:6]:
        copy.start()
    _, _, slot = routing(ids_ref[0, 0:1], ids_ref[0, 1:2], lax.axis_index("expert"))
    for arrived, leaving in ((0, 6), (1, 7)):
        copies[arrived].wait()
        copies[leaving].start()
    copies[2].wait()
    weight[2] = down[...].T
    copies[10].start()
    for arrived, leaving in ((3, 8), (4, 9)):
        copies[arrived].wait()
        copies[leaving].start()
    copies[5].wait()
    pack(rows[...], slot, slots, out_refs)
    for copy in copies[6:]:
        copy.wait()


def attend_kernel(
    slots, q_ref, k_ref, v_ref, past_ref, doc_ref, in_ref, gain_ref, ids_ref, att_ref, *refs
):
    out_refs, (resid_ref, squares_ref) = refs[:-2], refs[-2:]
    group, groups = pl.program_id(0), pl.num_programs(0)
    tok, part_width = q_ref.shape[1], q_ref.shape[2]
    here = lax.axis_index("expert")
    first = (here * lax.axis_size("ctx") + lax.axis_index("ctx")) * tok
    before = jnp.maximum(first - tok, 0)
    own_docs = doc_ref[:, pl.ds(pl.multiple_of(first, tok), tok)]
    past_docs = doc_ref[:, pl.ds(pl.multiple_of(before, tok), tok)]
    row = lax.broadcasted_iota(jnp.int32, (tok, tok), 0)
    col = lax.broadcasted_iota(jnp.int32, (tok, tok), 1)
    own_all = jnp.broadcast_to(own_docs, (tok, tok))
    query_docs = own_all.T
    see_own = (query_docs == own_all) & (col <= row)
    see_past = (query_docs == past_docs) & (first > 0)
    scale = HD ** (-0.5)
    squares = jnp.zeros((tok, HD), F32)
    for h in range(part_width // HD):
        at = slice(h * HD, (h + 1) * HD)
        q = q_ref[0, :, at]
        own = jnp.where(see_own, dot_t(q, k_ref[0, :, at]) * scale, -jnp.inf)
        past = jnp.where(see_past, dot_t(q, past_ref[0, :, at]) * scale, -jnp.inf)
        top = jnp.maximum(own, past).max(axis=1, keepdims=True)
        own, past = jnp.exp(own - top), jnp.exp(past - top)
        total = (own + past).sum(axis=1, keepdims=True)
        inverse = 1.0 / total
        own, past = (own * inverse).astype(BF), (past * inverse).astype(BF)
        part = dot(own, v_ref[0, :, at]) + dot(past, past_ref[1, :, at])
        part = part.astype(BF)
        att_ref[:, at] = part
        resid = in_ref[0, :, at].astype(F32) + part.astype(F32)
        resid_ref[group, :, at] = resid
        squares = squares + resid * resid

    @pl.when(group == 0)
    def _():
        squares_ref[...] = squares

    @pl.when(group > 0)
    def _():
        squares_ref[...] += squares

    @pl.when(group == groups - 1)
    def _():
        parts = resid_ref.shape[0]
        width = parts * part_width
        inv_rms = lax.rsqrt(squares_ref[...].sum(axis=1, keepdims=True) / width + 1e-06)
        _, _, slot = routing(ids_ref[0, 0:1], ids_ref[0, 1:2], here)
        table = placing_table(slot, slots, len(out_refs))
        for n in range(parts):
            at = slice(n * part_width, (n + 1) * part_width)
            normed = (resid_ref[n] * inv_rms * gain_ref[:, at]).astype(BF)
            packed = dot(table, normed).astype(BF)
            for k, out in enumerate(out_refs):
                out[:, at] = packed[k * slots : (k + 1) * slots]


def quarter(j, size):
    mine = lax.axis_index("fsdp") * lax.axis_size("ctx") + lax.axis_index("ctx")
    return pl.ds(pl.multiple_of((mine ^ j) * size, size), size)


def gather_rows(rows, slots, x):
    for j in range(x.shape[0]):
        at = quarter(j, x.shape[2])
        for k, block in enumerate(rows):
            x[j, k * slots : (k + 1) * slots] = block[:, at]


def summed(terms):
    total = terms[0]
    for term in terms[1:]:
        total = total + term
    return total


def hidden_kernel(count, pieces, *refs):
    rows, weights, refs = refs[:count], refs[count : count + pieces], refs[count + pieces :]
    hidden_ref, slope_ref, silu_ref, x = refs
    gather_rows(rows, rows[0].shape[0], x)
    step = 256
    for n in range(hidden_ref.shape[1] // step):
        at = slice(n * step, (n + 1) * step)
        gate_pre = summed([dot(x[j], weight[0, :, at]) for j, weight in enumerate(weights)])
        up_pre = summed([dot(x[j], weight[1, :, at]) for j, weight in enumerate(weights)])
        sig = 1.0 / (1.0 + jnp.exp(-gate_pre))
        silu = gate_pre * sig
        hidden_ref[:, at] = (silu * up_pre).astype(BF)
        slope_ref[:, at] = up_pre * sig * (1.0 + gate_pre * (1.0 - sig))
        silu_ref[:, at] = silu


def out_kernel(pieces, hidden_ref, *refs):
    weights, outs = refs[:pieces], refs[pieces:]
    slots = outs[0].shape[0]
    for j, weight in enumerate(weights):
        part = dot_t(hidden_ref[...], weight[2]).astype(BF)
        for k, out in enumerate(outs):
            out[:, quarter(j, weight.shape[1])] = part[k * slots : (k + 1) * slots]


def backward_kernel(rows_count, pieces, slots, *refs):
    rows, weights, refs = refs[:rows_count], refs[rows_count : rows_count + pieces], refs[rows_count + pieces :]
    slope_ref, silu_ref, refs = refs[0], refs[1], refs[2:]
    outs, (x, gate_grad, up_grad) = refs[:-3], refs[-3:]
    gather_rows(rows, slots, x)
    step = 256
    for n in range(gate_grad.shape[1] // step):
        at = slice(n * step, (n + 1) * step)
        hidden_grad = summed([dot(x[j], weight[2, :, at]) for j, weight in enumerate(weights)])
        gate_grad[:, at] = (hidden_grad * slope_ref[:, at]).astype(BF)
        up_grad[:, at] = (hidden_grad * silu_ref[:, at]).astype(BF)
    for j, weight in enumerate(weights):
        part = dot_t(gate_grad[...], weight[0]) + dot_t(up_grad[...], weight[1])
        part = part.astype(BF)
        for k, out in enumerate(outs):
            out[:, quarter(j, weight.shape[1])] = part[k * slots : (k + 1) * slots]


def mixed(ids_ref, weight_ref, backs, at, cache):
    if not cache:
        first, second, slot = routing(ids_ref[0, 0:1], ids_ref[0, 1:2], lax.axis_index("expert"))
        slots = backs[0].shape[0]
        gates = [column(weight_ref[0, j : j + 1]) for j in range(2)]
        for k in range(len(backs)):
            place = placing(slot, k, slots)[:, :slots].astype(BF)
            weight = jnp.where(first == k, gates[0], 0.0) + jnp.where(second == k, gates[1], 0.0)
            cache.append((place, weight))
    total = None
    for back, (place, weight) in zip(backs, cache):
        term = weight * dot(place, back[:, at])
        total = term if total is None else total + term
    return total


def layer_kernel(ids_ref, weight_ref, in_ref, att_ref, *refs):
    backs, out_ref = refs[:-1], refs[-1]
    step, cache = 512, []
    for n in range(in_ref.shape[2] // step):
        at = slice(n * step, (n + 1) * step)
        resid = in_ref[0, :, at].astype(F32) + att_ref[:, at].astype(F32)
        out_ref[0, :, at] = (resid + mixed(ids_ref, weight_ref, backs, at, cache)).astype(BF)


def grad_kernel(ids_ref, weight_ref, in_ref, att_ref, gain_ref, up_ref, *refs):
    backs, out_ref, gained_ref = refs[:-2], refs[-2], refs[-1]
    tok, width = in_ref.shape[1], in_ref.shape[2]
    step, cache = 512, []
    squares = jnp.zeros((tok, 1), F32)
    cross = jnp.zeros((tok, 1), F32)
    for n in range(width // step):
        at = slice(n * step, (n + 1) * step)
        resid = in_ref[0, :, at].astype(F32) + att_ref[:, at].astype(F32)
        gained = gain_ref[:, at] * mixed(ids_ref, weight_ref, backs, at, cache)
        gained_ref[:, at] = gained
        squares = squares + (resid * resid).sum(axis=1, keepdims=True)
        cross = cross + (resid * gained).sum(axis=1, keepdims=True)
    inv_rms = lax.rsqrt(squares / width + 1e-06)
    pull = inv_rms * inv_rms * inv_rms * (cross / width)
    for n in range(width // step):
        at = slice(n * step, (n + 1) * step)
        resid = in_ref[0, :, at].astype(F32) + att_ref[:, at].astype(F32)
        out_ref[0, :, at] = (
            up_ref[0, :, at].astype(F32) + inv_rms * gained_ref[:, at] - resid * pull
        ).astype(BF)


def shards(
    inputs, queries, keys, values, doc_ids, norm_gain, expert_ids, gate_weights, w_gate, w_up, w_down, out_grad
):
    tok, width = inputs.shape[1], inputs.shape[2]
    hidden_count = w_gate.shape[2]
    peers = lax.axis_size("expert")
    slots = 5 * tok // (2 * peers)
    slots = -(-slots // 16) * 16
    pieces = lax.axis_size("fsdp") * lax.axis_size("ctx")
    total = peers * slots
    slab = jax.ShapeDtypeStruct((slots, width), BF)
    slabs = [slab] * peers
    gain = norm_gain.reshape(1, width)
    ids, gates = jnp.swapaxes(expert_ids, 1, 2), jnp.swapaxes(gate_weights, 1, 2)


    def call(kernel, name, out_shape, count, scratch=(), mib=24):
        return pl.pallas_call(
            kernel,
            out_shape=out_shape,
            in_specs=[VM] * count,
            out_specs=[VM] * len(out_shape) if isinstance(out_shape, list) else VM,
            scratch_shapes=list(scratch),
            compiler_params=params(mib),
            name=name,
        )

    def exchanged(blocks):
        return [block if k == 0 else swapped(block, "expert", k) for k, block in enumerate(blocks)]

    def over_core(block):
        return swapped(block, "ctx", 1)

    def over_x(block):
        return [swapped(block, "fsdp", dx) for dx in range(1, lax.axis_size("fsdp"))]

    both, own_weights, *sent_grads = pl.pallas_call(
        lambda *refs: prepare_kernel(slots, *refs),
        out_shape=[
            jax.ShapeDtypeStruct((2, tok, width), BF),
            jax.ShapeDtypeStruct((3, w_gate.shape[1], hidden_count), BF),
        ]
        + slabs,
        in_specs=[VM] + [pl.BlockSpec(memory_space=pl.ANY)] * 6,
        out_specs=[pl.BlockSpec(memory_space=pl.ANY)] * 2 + [VM] * peers,
        scratch_shapes=[
            pltpu.VMEM((2, tok, width), BF),
            pltpu.VMEM((3, w_gate.shape[1], hidden_count), BF),
            pltpu.VMEM((tok, width), BF),
            pltpu.VMEM(w_down.shape[1:], BF),
            pltpu.SemaphoreType.DMA((11,)),
        ],
        compiler_params=params(56),
        name="prepare",
    )(ids, keys, values, out_grad, w_gate, w_up, w_down)
    previous = shifted(both, ("expert", "ctx"), 1)
    grads = exchanged([after(block, previous) for block in sent_grads[:-1]])
    weights_x = over_x(own_weights)

    parts = 4
    cut = width // parts

    def by_part(*dims):
        return pl.BlockSpec((*dims, cut), lambda n: (0,) * len(dims) + (n,))

    def fixed(*dims):
        return pl.BlockSpec(dims, lambda n: (0,) * len(dims))

    attended, *sent_rows = pl.pallas_call(
        lambda *refs: attend_kernel(slots, *refs),
        out_shape=[jax.ShapeDtypeStruct((tok, width), BF)] + slabs,
        grid=(parts,),
        in_specs=[by_part(1, tok)] * 3
        + [by_part(2, tok), fixed(*doc_ids.shape), by_part(1, tok), fixed(1, width), fixed(*ids.shape)],
        out_specs=[by_part(tok)] + [fixed(slots, width)] * peers,
        scratch_shapes=[pltpu.VMEM((parts, tok, cut), F32), pltpu.VMEM((tok, HD), F32)],
        compiler_params=params(16),
        name="attend",
    )(queries, keys, values, previous, doc_ids, inputs, gain, ids)
    rows = exchanged([after(block, grads[-1]) for block in sent_rows])

    weights = [own_weights, over_core(after(own_weights, attended))]
    for block in weights_x:
        weights += [block, over_core(after(block, *rows[1:]))]
    grads.append(swapped(after(sent_grads[-1], *rows[2:]), "expert", peers - 1))

    wide = jax.ShapeDtypeStruct((total, hidden_count), F32)
    x_scratch = pltpu.VMEM((pieces, total, w_gate.shape[1]), BF)
    hidden, slope, silu = call(
        lambda *refs: hidden_kernel(peers, pieces, *refs),
        "hidden",
        [jax.ShapeDtypeStruct((total, hidden_count), BF), wide, wide],
        peers + pieces,
        [x_scratch],
    )(*rows, *weights)
    served_out = call(lambda *refs: out_kernel(pieces, *refs), "served", slabs, 1 + pieces)(hidden, *weights)
    back_out = exchanged(served_out)

    served_grad = call(
        lambda *refs: backward_kernel(len(grads), pieces, slots, *refs),
        "backward",
        slabs,
        len(grads) + pieces + 2,
        [x_scratch] + [pltpu.VMEM((total, hidden_count), BF)] * 2,
    )(*grads, *weights, slope, silu)
    back_grad = exchanged(served_grad)

    out_block = jax.ShapeDtypeStruct(inputs.shape, BF)
    layer_out = pl.pallas_call(
        layer_kernel,
        out_shape=out_block,
        in_specs=[VM] * (4 + peers),
        out_specs=VM,
        compiler_params=params(32),
        name="layer",
    )(ids, gates, inputs, attended, *back_out)
    input_grad = pl.pallas_call(
        grad_kernel,
        out_shape=out_block,
        in_specs=[VM] * (6 + peers),
        out_specs=VM,
        scratch_shapes=[pltpu.VMEM((tok, width), F32)],
        compiler_params=params(32),
        name="grad",
    )(ids, gates, inputs, after(attended, layer_out), gain, out_grad, *back_grad)
    return layer_out, input_grad


def solution(mesh):
    rows = P(("groups", "fsdp"), ("expert", "ctx"), None)
    in_specs = (
        rows,
        rows,
        rows,
        rows,
        P(("groups", "fsdp"), None),
        P(),
        rows,
        rows,
        P("expert", ("fsdp", "ctx"), None),
        P("expert", ("fsdp", "ctx"), None),
        P("expert", None, ("fsdp", "ctx")),
        rows,
    )
    return jax.shard_map(shards, mesh=mesh, in_specs=in_specs, out_specs=(rows, rows), check_vma=False)
```

```python
import jax
import jax.numpy as jnp
from jax import lax
from jax.experimental import pallas as pl
from jax.experimental.pallas import tpu as pltpu
from jax.sharding import PartitionSpec as P

HEADS = 16
HD = 128
BF = jnp.bfloat16
F32 = jnp.float32
VM = pl.BlockSpec(memory_space=pltpu.VMEM)
MIB = 1024 * 1024


def params(mib):
    return pltpu.CompilerParams(vmem_limit_bytes=mib * MIB)


def swapped(block, axis, distance):
    count = lax.axis_size(axis)
    return lax.ppermute(block, axis, [(i, i ^ distance) for i in range(count)])


def shifted(block, axis, distance):
    devices = range(lax.axis_size(axis))
    route = [(i - distance, i) for i in devices if i - distance in devices]
    return lax.ppermute(block, axis, route)


def after(block, *others):
    return lax.optimization_barrier((block, *others))[0]


def dot(a, b):
    return jnp.dot(a, b, preferred_element_type=F32)


def dot_t(a, b):
    return lax.dot_general(a, b, (((1,), (1,)), ((), ())), preferred_element_type=F32)


def column(row):
    tok = row.shape[1]
    return jnp.broadcast_to(row, (tok, tok)).T[:, 0:1]


def routing(first, second, here):
    tok = first.shape[1]
    lane = lax.broadcasted_iota(jnp.int32, (tok, 128), 1)
    row = lax.broadcasted_iota(jnp.int32, (tok, tok), 0)
    col = lax.broadcasted_iota(jnp.int32, (tok, tok), 1)
    first, second = column(first) ^ here, column(second) ^ here
    chosen = (first == lane) | (second == lane)
    before = (col < row).astype(BF)
    rank = dot(before, chosen.astype(BF))
    slot = jnp.where(chosen, rank, -1.0)
    return first, second, slot


def placing(slot, k, slots):
    tok = slot.shape[0]
    lane = lax.broadcasted_iota(jnp.int32, (tok, 128), 1)
    return jnp.where(lane == slot[:, k : k + 1].astype(jnp.int32), 1.0, 0.0)


def placing_table(slot, slots, count):
    return jnp.concatenate([placing(slot, k, slots).T[:slots] for k in range(count)], 0).astype(BF)


def pack(rows, slot, slots, out_refs):
    packed = dot(placing_table(slot, slots, len(out_refs)), rows).astype(BF)
    for k, out in enumerate(out_refs):
        out[...] = packed[k * slots : (k + 1) * slots]


def prepare_kernel(u_hbm, d_hbm, weight_hbm, weight, down, sems):
    pairs = [
        (d_hbm.at[0], down),
        (u_hbm.at[0], weight.at[0]),
        (weight.at[0], weight_hbm.at[0]),
        (weight.at[1], weight_hbm.at[1]),
    ]
    copies = [pltpu.make_async_copy(source, target, sems.at[n]) for n, (source, target) in enumerate(pairs)]
    copies[0].start()
    copies[1].start()
    copies[1].wait()
    copies[2].start()
    copies[0].wait()
    weight[1] = down[...].T
    copies[3].start()
    copies[2].wait()
    copies[3].wait()


def pack_kernel(slots, ids_ref, rows_ref, *out_refs):
    _, _, slot = routing(ids_ref[0, 0:1], ids_ref[0, 1:2], lax.axis_index("expert"))
    pack(rows_ref[0], slot, slots, out_refs)


def attend_kernel(
    slots, q_ref, k_ref, v_ref, past_ref, doc_ref, in_ref, gain_ref, ids_ref, att_ref, *refs
):
    out_refs, (resid_ref, squares_ref) = refs[:-2], refs[-2:]
    group, groups = pl.program_id(0), pl.num_programs(0)
    tok, part_width = q_ref.shape[1], q_ref.shape[2]
    here = lax.axis_index("expert")
    first = (here * lax.axis_size("ctx") + lax.axis_index("ctx")) * tok
    before = jnp.maximum(first - tok, 0)
    own_docs = doc_ref[:, pl.ds(pl.multiple_of(first, tok), tok)]
    past_docs = doc_ref[:, pl.ds(pl.multiple_of(before, tok), tok)]
    row = lax.broadcasted_iota(jnp.int32, (tok, tok), 0)
    col = lax.broadcasted_iota(jnp.int32, (tok, tok), 1)
    own_all = jnp.broadcast_to(own_docs, (tok, tok))
    query_docs = own_all.T
    see_own = (query_docs == own_all) & (col <= row)
    see_past = (query_docs == past_docs) & (first > 0)
    scale = HD ** (-0.5)
    squares = jnp.zeros((tok, HD), F32)
    for h in range(part_width // HD):
        at = slice(h * HD, (h + 1) * HD)
        q = q_ref[0, :, at]
        own = jnp.where(see_own, dot_t(q, k_ref[0, :, at]) * scale, -jnp.inf)
        past = jnp.where(see_past, dot_t(q, past_ref[0, :, at]) * scale, -jnp.inf)
        top = jnp.maximum(own, past).max(axis=1, keepdims=True)
        own, past = jnp.exp(own - top), jnp.exp(past - top)
        total = (own + past).sum(axis=1, keepdims=True)
        inverse = 1.0 / total
        own, past = (own * inverse).astype(BF), (past * inverse).astype(BF)
        part = dot(own, v_ref[0, :, at]) + dot(past, past_ref[1, :, at])
        part = part.astype(BF)
        att_ref[:, at] = part
        resid = in_ref[0, :, at].astype(F32) + part.astype(F32)
        resid_ref[group, :, at] = resid
        squares = squares + resid * resid

    @pl.when(group == 0)
    def _():
        squares_ref[...] = squares

    @pl.when(group > 0)
    def _():
        squares_ref[...] += squares

    @pl.when(group == groups - 1)
    def _():
        parts = resid_ref.shape[0]
        width = parts * part_width
        inv_rms = lax.rsqrt(squares_ref[...].sum(axis=1, keepdims=True) / width + 1e-06)
        _, _, slot = routing(ids_ref[0, 0:1], ids_ref[0, 1:2], here)
        table = placing_table(slot, slots, len(out_refs))
        for n in range(parts):
            at = slice(n * part_width, (n + 1) * part_width)
            normed = (resid_ref[n] * inv_rms * gain_ref[:, at]).astype(BF)
            packed = dot(table, normed).astype(BF)
            for k, out in enumerate(out_refs):
                out[:, at] = packed[k * slots : (k + 1) * slots]


def quarter(j, size):
    mine = lax.axis_index("fsdp") * lax.axis_size("ctx") + lax.axis_index("ctx")
    return pl.ds(pl.multiple_of((mine ^ j) * size, size), size)


def gather_rows(rows, slots, x):
    for j in range(x.shape[0]):
        at = quarter(j, x.shape[2])
        for k, block in enumerate(rows):
            x[j, k * slots : (k + 1) * slots] = block[:, at]


def summed(terms):
    total = terms[0]
    for term in terms[1:]:
        total = total + term
    return total


def hidden_kernel(count, pieces, *refs):
    rows, gates, refs = refs[:count], refs[count : count + pieces], refs[count + pieces :]
    others, refs = refs[:pieces], refs[pieces:]
    hidden_ref, slope_ref, silu_ref, x = refs
    gather_rows(rows, rows[0].shape[0], x)
    step = 256
    for n in range(hidden_ref.shape[1] // step):
        at = slice(n * step, (n + 1) * step)
        gate_pre = summed([dot(x[j], gate[0, :, at]) for j, gate in enumerate(gates)])
        up_pre = summed([dot(x[j], other[0, :, at]) for j, other in enumerate(others)])
        sig = 1.0 / (1.0 + jnp.exp(-gate_pre))
        silu = gate_pre * sig
        hidden_ref[:, at] = (silu * up_pre).astype(BF)
        slope_ref[:, at] = up_pre * sig * (1.0 + gate_pre * (1.0 - sig))
        silu_ref[:, at] = silu


def out_kernel(pieces, hidden_ref, *refs):
    others, outs = refs[:pieces], refs[pieces:]
    slots = outs[0].shape[0]
    for j, other in enumerate(others):
        part = dot_t(hidden_ref[...], other[1]).astype(BF)
        for k, out in enumerate(outs):
            out[:, quarter(j, other.shape[1])] = part[k * slots : (k + 1) * slots]


def backward_kernel(rows_count, pieces, slots, *refs):
    rows, gates, refs = refs[:rows_count], refs[rows_count : rows_count + pieces], refs[rows_count + pieces :]
    others, slope_ref, silu_ref, refs = refs[:pieces], refs[pieces], refs[pieces + 1], refs[pieces + 2 :]
    outs, (x, gate_grad, up_grad) = refs[:-3], refs[-3:]
    gather_rows(rows, slots, x)
    step = 256
    for n in range(gate_grad.shape[1] // step):
        at = slice(n * step, (n + 1) * step)
        hidden_grad = summed([dot(x[j], other[1, :, at]) for j, other in enumerate(others)])
        gate_grad[:, at] = (hidden_grad * slope_ref[:, at]).astype(BF)
        up_grad[:, at] = (hidden_grad * silu_ref[:, at]).astype(BF)
    for j, (gate, other) in enumerate(zip(gates, others)):
        part = dot_t(gate_grad[...], gate[0]) + dot_t(up_grad[...], other[0])
        part = part.astype(BF)
        for k, out in enumerate(outs):
            out[:, quarter(j, gate.shape[1])] = part[k * slots : (k + 1) * slots]


def mixed(ids_ref, weight_ref, backs, at, cache):
    if not cache:
        first, second, slot = routing(ids_ref[0, 0:1], ids_ref[0, 1:2], lax.axis_index("expert"))
        slots = backs[0].shape[0]
        gates = [column(weight_ref[0, j : j + 1]) for j in range(2)]
        for k in range(len(backs)):
            place = placing(slot, k, slots)[:, :slots].astype(BF)
            weight = jnp.where(first == k, gates[0], 0.0) + jnp.where(second == k, gates[1], 0.0)
            cache.append((place, weight))
    total = None
    for back, (place, weight) in zip(backs, cache):
        term = weight * dot(place, back[:, at])
        total = term if total is None else total + term
    return total


def layer_kernel(ids_ref, weight_ref, in_ref, att_ref, *refs):
    backs, out_ref = refs[:-1], refs[-1]
    step, cache = 512, []
    for n in range(in_ref.shape[2] // step):
        at = slice(n * step, (n + 1) * step)
        resid = in_ref[0, :, at].astype(F32) + att_ref[:, at].astype(F32)
        out_ref[0, :, at] = (resid + mixed(ids_ref, weight_ref, backs, at, cache)).astype(BF)


def grad_kernel(ids_ref, weight_ref, in_ref, att_ref, gain_ref, up_ref, *refs):
    backs, out_ref, gained_ref = refs[:-2], refs[-2], refs[-1]
    tok, width = in_ref.shape[1], in_ref.shape[2]
    step, cache = 512, []
    squares = jnp.zeros((tok, 1), F32)
    cross = jnp.zeros((tok, 1), F32)
    for n in range(width // step):
        at = slice(n * step, (n + 1) * step)
        resid = in_ref[0, :, at].astype(F32) + att_ref[:, at].astype(F32)
        gained = gain_ref[:, at] * mixed(ids_ref, weight_ref, backs, at, cache)
        gained_ref[:, at] = gained
        squares = squares + (resid * resid).sum(axis=1, keepdims=True)
        cross = cross + (resid * gained).sum(axis=1, keepdims=True)
    inv_rms = lax.rsqrt(squares / width + 1e-06)
    pull = inv_rms * inv_rms * inv_rms * (cross / width)
    for n in range(width // step):
        at = slice(n * step, (n + 1) * step)
        resid = in_ref[0, :, at].astype(F32) + att_ref[:, at].astype(F32)
        out_ref[0, :, at] = (
            up_ref[0, :, at].astype(F32) + inv_rms * gained_ref[:, at] - resid * pull
        ).astype(BF)


def shards(
    inputs, queries, keys, values, doc_ids, norm_gain, expert_ids, gate_weights, w_gate, w_up, w_down, out_grad
):
    tok, width = inputs.shape[1], inputs.shape[2]
    hidden_count = w_gate.shape[2]
    peers = lax.axis_size("expert")
    slots = 5 * tok // (2 * peers)
    slots = -(-slots // 16) * 16
    pieces = lax.axis_size("fsdp") * lax.axis_size("ctx")
    total = peers * slots
    slab = jax.ShapeDtypeStruct((slots, width), BF)
    slabs = [slab] * peers
    gain = norm_gain.reshape(1, width)
    ids, gates = jnp.swapaxes(expert_ids, 1, 2), jnp.swapaxes(gate_weights, 1, 2)


    def call(kernel, name, out_shape, count, scratch=(), mib=24):
        return pl.pallas_call(
            kernel,
            out_shape=out_shape,
            in_specs=[VM] * count,
            out_specs=[VM] * len(out_shape) if isinstance(out_shape, list) else VM,
            scratch_shapes=list(scratch),
            compiler_params=params(mib),
            name=name,
        )

    def exchanged(blocks):
        return [block if k == 0 else swapped(block, "expert", k) for k, block in enumerate(blocks)]

    def over_core(block):
        return swapped(block, "ctx", 1)

    def over_x(block):
        return [swapped(block, "fsdp", dx) for dx in range(1, lax.axis_size("fsdp"))]

    both = jnp.concatenate([keys, values], 0)
    previous = shifted(both, ("expert", "ctx"), 1)
    own_others = pl.pallas_call(
        prepare_kernel,
        out_shape=jax.ShapeDtypeStruct((2, w_gate.shape[1], hidden_count), BF),
        in_specs=[pl.BlockSpec(memory_space=pl.ANY)] * 2,
        out_specs=pl.BlockSpec(memory_space=pl.ANY),
        scratch_shapes=[
            pltpu.VMEM((2, w_gate.shape[1], hidden_count), BF),
            pltpu.VMEM(w_down.shape[1:], BF),
            pltpu.SemaphoreType.DMA((4,)),
        ],
        compiler_params=params(56),
        name="prepare",
    )(w_up, after(w_down, both))
    sent_grads = call(lambda *refs: pack_kernel(slots, *refs), "pack_grad", slabs, 2)(ids, after(out_grad, own_others))
    grads = [
        block if k < 2 else swapped(after(block, previous), "expert", k) for k, block in enumerate(sent_grads[:-1])
    ]
    gates_x, others_x = over_x(w_gate), over_x(own_others)

    parts = 4
    cut = width // parts

    def by_part(*dims):
        return pl.BlockSpec((*dims, cut), lambda n: (0,) * len(dims) + (n,))

    def fixed(*dims):
        return pl.BlockSpec(dims, lambda n: (0,) * len(dims))

    attended, *sent_rows = pl.pallas_call(
        lambda *refs: attend_kernel(slots, *refs),
        out_shape=[jax.ShapeDtypeStruct((tok, width), BF)] + slabs,
        grid=(parts,),
        in_specs=[by_part(1, tok)] * 3
        + [by_part(2, tok), fixed(*doc_ids.shape), by_part(1, tok), fixed(1, width), fixed(*ids.shape)],
        out_specs=[by_part(tok)] + [fixed(slots, width)] * peers,
        scratch_shapes=[pltpu.VMEM((parts, tok, cut), F32), pltpu.VMEM((tok, HD), F32)],
        compiler_params=params(16),
        name="attend",
    )(queries, keys, values, previous, doc_ids, inputs, gain, ids)
    rows = exchanged([after(block, grads[-1]) for block in sent_rows])

    all_gates, all_others = [w_gate, over_core(after(w_gate, attended))], [own_others, over_core(after(own_others, attended))]
    for gate, other in zip(gates_x, others_x):
        all_gates += [gate, over_core(after(gate, *rows[1:]))]
        all_others += [other, over_core(after(other, *rows[1:]))]
    grads.append(swapped(after(sent_grads[-1], *rows[2:]), "expert", peers - 1))

    wide = jax.ShapeDtypeStruct((total, hidden_count), F32)
    x_scratch = pltpu.VMEM((pieces, total, w_gate.shape[1]), BF)
    hidden, slope, silu = call(
        lambda *refs: hidden_kernel(peers, pieces, *refs),
        "hidden",
        [jax.ShapeDtypeStruct((total, hidden_count), BF), wide, wide],
        peers + 2 * pieces,
        [x_scratch],
    )(*rows, *all_gates, *all_others)
    grads[1] = swapped(after(grads[1], hidden), "expert", 1)
    served_out = call(lambda *refs: out_kernel(pieces, *refs), "served", slabs, 1 + pieces)(hidden, *all_others)
    back_out = exchanged(served_out)

    served_grad = call(
        lambda *refs: backward_kernel(len(grads), pieces, slots, *refs),
        "backward",
        slabs,
        len(grads) + 2 * pieces + 2,
        [x_scratch] + [pltpu.VMEM((total, hidden_count), BF)] * 2,
    )(*grads, *all_gates, *all_others, slope, silu)
    back_grad = exchanged(served_grad)

    out_block = jax.ShapeDtypeStruct(inputs.shape, BF)
    layer_out = pl.pallas_call(
        layer_kernel,
        out_shape=out_block,
        in_specs=[VM] * (4 + peers),
        out_specs=VM,
        compiler_params=params(32),
        name="layer",
    )(ids, gates, inputs, attended, *back_out)
    input_grad = pl.pallas_call(
        grad_kernel,
        out_shape=out_block,
        in_specs=[VM] * (6 + peers),
        out_specs=VM,
        scratch_shapes=[pltpu.VMEM((tok, width), F32)],
        compiler_params=params(32),
        name="grad",
    )(ids, gates, inputs, after(attended, layer_out), gain, out_grad, *back_grad)
    return layer_out, input_grad


def solution(mesh):
    rows = P(("groups", "fsdp"), ("expert", "ctx"), None)
    in_specs = (
        rows,
        rows,
        rows,
        rows,
        P(("groups", "fsdp"), None),
        P(),
        rows,
        rows,
        P("expert", ("fsdp", "ctx"), None),
        P("expert", ("fsdp", "ctx"), None),
        P("expert", None, ("fsdp", "ctx")),
        rows,
    )
    return jax.shard_map(shards, mesh=mesh, in_specs=in_specs, out_specs=(rows, rows), check_vma=False)
```

```python
import jax
import jax.numpy as jnp
from jax import lax
from jax.experimental import pallas as pl
from jax.experimental.pallas import tpu as pltpu
from jax.sharding import PartitionSpec as P

HEADS = 16
HD = 128
BF = jnp.bfloat16
F32 = jnp.float32
VM = pl.BlockSpec(memory_space=pltpu.VMEM)
MIB = 1024 * 1024


def params(mib):
    return pltpu.CompilerParams(vmem_limit_bytes=mib * MIB)


def swapped(block, axis, distance):
    count = lax.axis_size(axis)
    return lax.ppermute(block, axis, [(i, i ^ distance) for i in range(count)])


def shifted(block, axis, distance):
    devices = range(lax.axis_size(axis))
    route = [(i - distance, i) for i in devices if i - distance in devices]
    return lax.ppermute(block, axis, route)


def after(block, *others):
    return lax.optimization_barrier((block, *others))[0]


def dot(a, b):
    return jnp.dot(a, b, preferred_element_type=F32)


def dot_t(a, b):
    return lax.dot_general(a, b, (((1,), (1,)), ((), ())), preferred_element_type=F32)


def column(row):
    tok = row.shape[1]
    return jnp.broadcast_to(row, (tok, tok)).T[:, 0:1]


def routing(first, second, here):
    tok = first.shape[1]
    lane = lax.broadcasted_iota(jnp.int32, (tok, 128), 1)
    row = lax.broadcasted_iota(jnp.int32, (tok, tok), 0)
    col = lax.broadcasted_iota(jnp.int32, (tok, tok), 1)
    first, second = column(first) ^ here, column(second) ^ here
    chosen = (first == lane) | (second == lane)
    before = (col < row).astype(BF)
    rank = dot(before, chosen.astype(BF))
    slot = jnp.where(chosen, rank, -1.0)
    return first, second, slot


def placing(slot, k, slots):
    tok = slot.shape[0]
    lane = lax.broadcasted_iota(jnp.int32, (tok, 128), 1)
    return jnp.where(lane == slot[:, k : k + 1].astype(jnp.int32), 1.0, 0.0)


def placing_table(slot, slots, count):
    return jnp.concatenate([placing(slot, k, slots).T[:slots] for k in range(count)], 0).astype(BF)


def pack(rows, slot, slots, out_refs):
    packed = dot(placing_table(slot, slots, len(out_refs)), rows).astype(BF)
    for k, out in enumerate(out_refs):
        out[...] = packed[k * slots : (k + 1) * slots]


def prepare_kernel(u_hbm, d_hbm, weight_hbm, weight, down, sems):
    pairs = [
        (d_hbm.at[0], down),
        (u_hbm.at[0], weight.at[0]),
        (weight.at[0], weight_hbm.at[0]),
        (weight.at[1], weight_hbm.at[1]),
    ]
    copies = [pltpu.make_async_copy(source, target, sems.at[n]) for n, (source, target) in enumerate(pairs)]
    copies[0].start()
    copies[1].start()
    copies[1].wait()
    copies[2].start()
    copies[0].wait()
    weight[1] = down[...].T
    copies[3].start()
    copies[2].wait()
    copies[3].wait()


def pack_kernel(slots, ids_ref, rows_ref, *out_refs):
    _, _, slot = routing(ids_ref[0, 0:1], ids_ref[0, 1:2], lax.axis_index("expert"))
    pack(rows_ref[0], slot, slots, out_refs)


def attend_kernel(
    slots, q_ref, k_ref, v_ref, kp_ref, vp_ref, doc_ref, in_ref, gain_ref, ids_ref, att_ref, *refs
):
    out_refs, (resid_ref, squares_ref) = refs[:-2], refs[-2:]
    group, groups = pl.program_id(0), pl.num_programs(0)
    tok, part_width = q_ref.shape[1], q_ref.shape[2]
    here = lax.axis_index("expert")
    first = (here * lax.axis_size("ctx") + lax.axis_index("ctx")) * tok
    before = jnp.maximum(first - tok, 0)
    own_docs = doc_ref[:, pl.ds(pl.multiple_of(first, tok), tok)]
    past_docs = doc_ref[:, pl.ds(pl.multiple_of(before, tok), tok)]
    row = lax.broadcasted_iota(jnp.int32, (tok, tok), 0)
    col = lax.broadcasted_iota(jnp.int32, (tok, tok), 1)
    own_all = jnp.broadcast_to(own_docs, (tok, tok))
    query_docs = own_all.T
    see_own = (query_docs == own_all) & (col <= row)
    see_past = (query_docs == past_docs) & (first > 0)
    scale = HD ** (-0.5)
    squares = jnp.zeros((tok, HD), F32)
    for h in range(part_width // HD):
        at = slice(h * HD, (h + 1) * HD)
        q = q_ref[0, :, at]
        own = jnp.where(see_own, dot_t(q, k_ref[0, :, at]) * scale, -jnp.inf)
        past = jnp.where(see_past, dot_t(q, kp_ref[0, :, at]) * scale, -jnp.inf)
        top = jnp.maximum(own, past).max(axis=1, keepdims=True)
        own, past = jnp.exp(own - top), jnp.exp(past - top)
        total = (own + past).sum(axis=1, keepdims=True)
        inverse = 1.0 / total
        own, past = (own * inverse).astype(BF), (past * inverse).astype(BF)
        part = dot(own, v_ref[0, :, at]) + dot(past, vp_ref[0, :, at])
        part = part.astype(BF)
        att_ref[:, at] = part
        resid = in_ref[0, :, at].astype(F32) + part.astype(F32)
        resid_ref[group, :, at] = resid
        squares = squares + resid * resid

    @pl.when(group == 0)
    def _():
        squares_ref[...] = squares

    @pl.when(group > 0)
    def _():
        squares_ref[...] += squares

    @pl.when(group == groups - 1)
    def _():
        parts = resid_ref.shape[0]
        width = parts * part_width
        inv_rms = lax.rsqrt(squares_ref[...].sum(axis=1, keepdims=True) / width + 1e-06)
        _, _, slot = routing(ids_ref[0, 0:1], ids_ref[0, 1:2], here)
        table = placing_table(slot, slots, len(out_refs))
        for n in range(parts):
            at = slice(n * part_width, (n + 1) * part_width)
            normed = (resid_ref[n] * inv_rms * gain_ref[:, at]).astype(BF)
            packed = dot(table, normed).astype(BF)
            for k, out in enumerate(out_refs):
                out[:, at] = packed[k * slots : (k + 1) * slots]


def quarter(j, size):
    mine = lax.axis_index("fsdp") * lax.axis_size("ctx") + lax.axis_index("ctx")
    return pl.ds(pl.multiple_of((mine ^ j) * size, size), size)


def gather_rows(rows, slots, x):
    for j in range(x.shape[0]):
        at = quarter(j, x.shape[2])
        for k, block in enumerate(rows):
            x[j, k * slots : (k + 1) * slots] = block[:, at]


def summed(terms):
    total = terms[0]
    for term in terms[1:]:
        total = total + term
    return total


def hidden_kernel(count, pieces, *refs):
    rows, gates, refs = refs[:count], refs[count : count + pieces], refs[count + pieces :]
    others, refs = refs[:pieces], refs[pieces:]
    hidden_ref, slope_ref, silu_ref, x = refs
    gather_rows(rows, rows[0].shape[0], x)
    step = 256
    for n in range(hidden_ref.shape[1] // step):
        at = slice(n * step, (n + 1) * step)
        gate_pre = summed([dot(x[j], gate[0, :, at]) for j, gate in enumerate(gates)])
        up_pre = summed([dot(x[j], other[0, :, at]) for j, other in enumerate(others)])
        sig = 1.0 / (1.0 + jnp.exp(-gate_pre))
        silu = gate_pre * sig
        hidden_ref[:, at] = (silu * up_pre).astype(BF)
        slope_ref[:, at] = up_pre * sig * (1.0 + gate_pre * (1.0 - sig))
        silu_ref[:, at] = silu


def out_kernel(pieces, hidden_ref, *refs):
    others, outs = refs[:pieces], refs[pieces:]
    slots = outs[0].shape[0]
    for j, other in enumerate(others):
        part = dot_t(hidden_ref[...], other[1]).astype(BF)
        for k, out in enumerate(outs):
            out[:, quarter(j, other.shape[1])] = part[k * slots : (k + 1) * slots]


def backward_kernel(rows_count, pieces, slots, *refs):
    rows, gates, refs = refs[:rows_count], refs[rows_count : rows_count + pieces], refs[rows_count + pieces :]
    others, slope_ref, silu_ref, refs = refs[:pieces], refs[pieces], refs[pieces + 1], refs[pieces + 2 :]
    outs, (x, gate_grad, up_grad) = refs[:-3], refs[-3:]
    gather_rows(rows, slots, x)
    step = 256
    for n in range(gate_grad.shape[1] // step):
        at = slice(n * step, (n + 1) * step)
        hidden_grad = summed([dot(x[j], other[1, :, at]) for j, other in enumerate(others)])
        gate_grad[:, at] = (hidden_grad * slope_ref[:, at]).astype(BF)
        up_grad[:, at] = (hidden_grad * silu_ref[:, at]).astype(BF)
    for j, (gate, other) in enumerate(zip(gates, others)):
        part = dot_t(gate_grad[...], gate[0]) + dot_t(up_grad[...], other[0])
        part = part.astype(BF)
        for k, out in enumerate(outs):
            out[:, quarter(j, gate.shape[1])] = part[k * slots : (k + 1) * slots]


def mixed(ids_ref, weight_ref, backs, kinds, at, cache):
    if not cache:
        first, second, slot = routing(ids_ref[0, 0:1], ids_ref[0, 1:2], lax.axis_index("expert"))
        slots = backs[0].shape[0]
        gates = [column(weight_ref[0, j : j + 1]) for j in range(2)]
        for k in kinds:
            place = placing(slot, k, slots)[:, :slots].astype(BF)
            weight = jnp.where(first == k, gates[0], 0.0) + jnp.where(second == k, gates[1], 0.0)
            cache.append((place, weight))
    return summed([weight * dot(place, back[:, at]) for back, (place, weight) in zip(backs, cache)])


def layer_kernel(ids_ref, weight_ref, in_ref, att_ref, *refs):
    backs, out_ref = refs[:-1], refs[-1]
    step, cache = 512, []
    for n in range(in_ref.shape[2] // step):
        at = slice(n * step, (n + 1) * step)
        resid = in_ref[0, :, at].astype(F32) + att_ref[:, at].astype(F32)
        out_ref[0, :, at] = (resid + mixed(ids_ref, weight_ref, backs, range(len(backs)), at, cache)).astype(BF)


def near_grad_kernel(ids_ref, weight_ref, in_ref, att_ref, *refs):
    backs, sum_ref, rms_ref = refs[:-2], refs[-2], refs[-1]
    tok, width = in_ref.shape[1], in_ref.shape[2]
    step, cache = 512, []
    squares = jnp.zeros((tok, 1), F32)
    for n in range(width // step):
        at = slice(n * step, (n + 1) * step)
        resid = in_ref[0, :, at].astype(F32) + att_ref[:, at].astype(F32)
        sum_ref[:, at] = mixed(ids_ref, weight_ref, backs, range(len(backs)), at, cache)
        squares = squares + (resid * resid).sum(axis=1, keepdims=True)
    rms_ref[...] = jnp.broadcast_to(lax.rsqrt(squares / width + 1e-06), rms_ref.shape)


def grad_kernel(ids_ref, weight_ref, in_ref, att_ref, gain_ref, up_ref, sum_ref, rms_ref, *refs):
    backs, out_ref, gained_ref = refs[:-2], refs[-2], refs[-1]
    tok, width = in_ref.shape[1], in_ref.shape[2]
    step, cache = 512, []
    kinds = range(lax.axis_size("expert") - len(backs), lax.axis_size("expert"))
    cross = jnp.zeros((tok, 1), F32)
    for n in range(width // step):
        at = slice(n * step, (n + 1) * step)
        resid = in_ref[0, :, at].astype(F32) + att_ref[:, at].astype(F32)
        gained = gain_ref[:, at] * (sum_ref[:, at] + mixed(ids_ref, weight_ref, backs, kinds, at, cache))
        gained_ref[:, at] = gained
        cross = cross + (resid * gained).sum(axis=1, keepdims=True)
    inv_rms = rms_ref[:, 0:1]
    pull = inv_rms * inv_rms * inv_rms * (cross / width)
    for n in range(width // step):
        at = slice(n * step, (n + 1) * step)
        resid = in_ref[0, :, at].astype(F32) + att_ref[:, at].astype(F32)
        out_ref[0, :, at] = (
            up_ref[0, :, at].astype(F32) + inv_rms * gained_ref[:, at] - resid * pull
        ).astype(BF)


def shards(
    inputs, queries, keys, values, doc_ids, norm_gain, expert_ids, gate_weights, w_gate, w_up, w_down, out_grad
):
    tok, width = inputs.shape[1], inputs.shape[2]
    hidden_count = w_gate.shape[2]
    peers = lax.axis_size("expert")
    slots = 5 * tok // (2 * peers)
    slots = -(-slots // 16) * 16
    pieces = lax.axis_size("fsdp") * lax.axis_size("ctx")
    total = peers * slots
    slab = jax.ShapeDtypeStruct((slots, width), BF)
    slabs = [slab] * peers
    gain = norm_gain.reshape(1, width)
    ids, gates = jnp.swapaxes(expert_ids, 1, 2), jnp.swapaxes(gate_weights, 1, 2)


    def call(kernel, name, out_shape, count, scratch=(), mib=24):
        return pl.pallas_call(
            kernel,
            out_shape=out_shape,
            in_specs=[VM] * count,
            out_specs=[VM] * len(out_shape) if isinstance(out_shape, list) else VM,
            scratch_shapes=list(scratch),
            compiler_params=params(mib),
            name=name,
        )

    def exchanged(blocks):
        return [block if k == 0 else swapped(block, "expert", k) for k, block in enumerate(blocks)]

    def over_core(block):
        return swapped(block, "ctx", 1)

    def over_x(block):
        return [swapped(block, "fsdp", dx) for dx in range(1, lax.axis_size("fsdp"))]

    both = jnp.concatenate([keys, values], 2)
    previous = shifted(both, ("expert", "ctx"), 1)
    own_others = pl.pallas_call(
        prepare_kernel,
        out_shape=jax.ShapeDtypeStruct((2, w_gate.shape[1], hidden_count), BF),
        in_specs=[pl.BlockSpec(memory_space=pl.ANY)] * 2,
        out_specs=pl.BlockSpec(memory_space=pl.ANY),
        scratch_shapes=[
            pltpu.VMEM((2, w_gate.shape[1], hidden_count), BF),
            pltpu.VMEM(w_down.shape[1:], BF),
            pltpu.SemaphoreType.DMA((4,)),
        ],
        compiler_params=params(56),
        name="prepare",
    )(w_up, after(w_down, both))
    sent_grads = call(lambda *refs: pack_kernel(slots, *refs), "pack_grad", slabs, 2)(ids, after(out_grad, own_others))
    grads = [
        block if k < 2 else swapped(after(block, previous), "expert", k) for k, block in enumerate(sent_grads[:-1])
    ]
    gates_x, others_x = over_x(w_gate), over_x(own_others)

    parts = 4
    cut = width // parts

    def by_part(*dims):
        return pl.BlockSpec((*dims, cut), lambda n: (0,) * len(dims) + (n,))

    def fixed(*dims):
        return pl.BlockSpec(dims, lambda n: (0,) * len(dims))

    attended, *sent_rows = pl.pallas_call(
        lambda *refs: attend_kernel(slots, *refs),
        out_shape=[jax.ShapeDtypeStruct((tok, width), BF)] + slabs,
        grid=(parts,),
        in_specs=[by_part(1, tok)] * 3
        + [by_part(1, tok), pl.BlockSpec((1, tok, cut), lambda n: (0, 0, n + parts)), fixed(*doc_ids.shape), by_part(1, tok), fixed(1, width), fixed(*ids.shape)],
        out_specs=[by_part(tok)] + [fixed(slots, width)] * peers,
        scratch_shapes=[pltpu.VMEM((parts, tok, cut), F32), pltpu.VMEM((tok, HD), F32)],
        compiler_params=params(16),
        name="attend",
    )(queries, keys, values, previous, previous, doc_ids, inputs, gain, ids)
    rows = exchanged([after(block, grads[-1]) for block in sent_rows])

    all_gates, all_others = [w_gate, over_core(after(w_gate, attended))], [own_others, over_core(after(own_others, attended))]
    for gate, other in zip(gates_x, others_x):
        all_gates += [gate, over_core(after(gate, *rows[1:]))]
        all_others += [other, over_core(after(other, *rows[1:]))]
    grads.append(swapped(after(sent_grads[-1], *rows[2:]), "expert", peers - 1))

    wide = jax.ShapeDtypeStruct((total, hidden_count), F32)
    x_scratch = pltpu.VMEM((pieces, total, w_gate.shape[1]), BF)
    hidden, slope, silu = call(
        lambda *refs: hidden_kernel(peers, pieces, *refs),
        "hidden",
        [jax.ShapeDtypeStruct((total, hidden_count), BF), wide, wide],
        peers + 2 * pieces,
        [x_scratch],
    )(*rows, *all_gates, *all_others)
    grads[1] = swapped(after(grads[1], hidden), "expert", 1)
    served_out = call(lambda *refs: out_kernel(pieces, *refs), "served", slabs, 1 + pieces)(hidden, *all_others)
    back_out = exchanged(served_out)

    served_grad = call(
        lambda *refs: backward_kernel(len(grads), pieces, slots, *refs),
        "backward",
        slabs,
        len(grads) + 2 * pieces + 2,
        [x_scratch] + [pltpu.VMEM((total, hidden_count), BF)] * 2,
    )(*grads, *all_gates, *all_others, slope, silu)
    back_grad = exchanged(served_grad)

    out_block = jax.ShapeDtypeStruct(inputs.shape, BF)
    layer_out = pl.pallas_call(
        layer_kernel,
        out_shape=out_block,
        in_specs=[VM] * (4 + peers),
        out_specs=VM,
        compiler_params=params(32),
        name="layer",
    )(ids, gates, inputs, attended, *back_out)
    near = peers - 1
    near_sum, inv_rms = call(
        near_grad_kernel,
        "near_grad",
        [jax.ShapeDtypeStruct((tok, width), F32), jax.ShapeDtypeStruct((tok, 128), F32)],
        4 + near,
    )(ids, gates, inputs, after(attended, layer_out), *back_grad[:near])
    input_grad = call(
        grad_kernel, "grad", out_block, 8 + peers - near, [pltpu.VMEM((tok, width), F32)]
    )(ids, gates, inputs, attended, gain, out_grad, near_sum, inv_rms, *back_grad[near:])
    return layer_out, input_grad


def solution(mesh):
    rows = P(("groups", "fsdp"), ("expert", "ctx"), None)
    in_specs = (
        rows,
        rows,
        rows,
        rows,
        P(("groups", "fsdp"), None),
        P(),
        rows,
        rows,
        P("expert", ("fsdp", "ctx"), None),
        P("expert", ("fsdp", "ctx"), None),
        P("expert", None, ("fsdp", "ctx")),
        rows,
    )
    return jax.shard_map(shards, mesh=mesh, in_specs=in_specs, out_specs=(rows, rows), check_vma=False)
```

```python
import jax
import jax.numpy as jnp
from jax import lax
from jax.experimental import pallas as pl
from jax.experimental.pallas import tpu as pltpu
from jax.sharding import PartitionSpec as P

HEADS = 16
HD = 128
BF = jnp.bfloat16
F32 = jnp.float32
VM = pl.BlockSpec(memory_space=pltpu.VMEM)
MIB = 1024 * 1024


def params(mib):
    return pltpu.CompilerParams(vmem_limit_bytes=mib * MIB)


def swapped(block, axis, distance):
    count = lax.axis_size(axis)
    return lax.ppermute(block, axis, [(i, i ^ distance) for i in range(count)])


def shifted(block, axis, distance):
    devices = range(lax.axis_size(axis))
    route = [(i - distance, i) for i in devices if i - distance in devices]
    return lax.ppermute(block, axis, route)


def after(block, *others):
    return lax.optimization_barrier((block, *others))[0]


def dot(a, b):
    return jnp.dot(a, b, preferred_element_type=F32)


def dot_t(a, b):
    return lax.dot_general(a, b, (((1,), (1,)), ((), ())), preferred_element_type=F32)


def column(row):
    tok = row.shape[1]
    return jnp.broadcast_to(row, (tok, tok)).T[:, 0:1]


def routing(first, second, here):
    tok = first.shape[1]
    lane = lax.broadcasted_iota(jnp.int32, (tok, 128), 1)
    row = lax.broadcasted_iota(jnp.int32, (tok, tok), 0)
    col = lax.broadcasted_iota(jnp.int32, (tok, tok), 1)
    first, second = column(first) ^ here, column(second) ^ here
    chosen = (first == lane) | (second == lane)
    before = (col < row).astype(BF)
    rank = dot(before, chosen.astype(BF))
    slot = jnp.where(chosen, rank, -1.0)
    return first, second, slot


def placing(slot, k, slots):
    tok = slot.shape[0]
    lane = lax.broadcasted_iota(jnp.int32, (tok, 128), 1)
    return jnp.where(lane == slot[:, k : k + 1].astype(jnp.int32), 1.0, 0.0)


def placing_table(slot, slots, count):
    return jnp.concatenate([placing(slot, k, slots).T[:slots] for k in range(count)], 0).astype(BF)


def pack(rows, slot, slots, out_refs):
    packed = dot(placing_table(slot, slots, len(out_refs)), rows).astype(BF)
    for k, out in enumerate(out_refs):
        out[...] = packed[k * slots : (k + 1) * slots]


def prepare_kernel(u_hbm, d_hbm, weight_hbm, weight, down, sems):
    pairs = [
        (d_hbm.at[0], down),
        (u_hbm.at[0], weight.at[0]),
        (weight.at[0], weight_hbm.at[0]),
        (weight.at[1], weight_hbm.at[1]),
    ]
    copies = [pltpu.make_async_copy(source, target, sems.at[n]) for n, (source, target) in enumerate(pairs)]
    copies[0].start()
    copies[1].start()
    copies[1].wait()
    copies[2].start()
    copies[0].wait()
    weight[1] = down[...].T
    copies[3].start()
    copies[2].wait()
    copies[3].wait()


def pack_kernel(slots, ids_ref, rows_ref, *out_refs):
    _, _, slot = routing(ids_ref[0, 0:1], ids_ref[0, 1:2], lax.axis_index("expert"))
    pack(rows_ref[0], slot, slots, out_refs)


def attend_kernel(
    slots, q_ref, k_ref, v_ref, kp_ref, vp_ref, doc_ref, in_ref, gain_ref, ids_ref, att_ref, *refs
):
    out_refs, (resid_ref, squares_ref) = refs[:-2], refs[-2:]
    group, groups = pl.program_id(0), pl.num_programs(0)
    tok, part_width = q_ref.shape[1], q_ref.shape[2]
    here = lax.axis_index("expert")
    first = (here * lax.axis_size("ctx") + lax.axis_index("ctx")) * tok
    before = jnp.maximum(first - tok, 0)
    own_docs = doc_ref[:, pl.ds(pl.multiple_of(first, tok), tok)]
    past_docs = doc_ref[:, pl.ds(pl.multiple_of(before, tok), tok)]
    row = lax.broadcasted_iota(jnp.int32, (tok, tok), 0)
    col = lax.broadcasted_iota(jnp.int32, (tok, tok), 1)
    own_all = jnp.broadcast_to(own_docs, (tok, tok))
    query_docs = own_all.T
    see_own = (query_docs == own_all) & (col <= row)
    see_past = (query_docs == past_docs) & (first > 0)
    scale = HD ** (-0.5)
    squares = jnp.zeros((tok, HD), F32)
    for h in range(part_width // HD):
        at = slice(h * HD, (h + 1) * HD)
        q = q_ref[0, :, at]
        own = jnp.where(see_own, dot_t(q, k_ref[0, :, at]) * scale, -jnp.inf)
        past = jnp.where(see_past, dot_t(q, kp_ref[0, :, at]) * scale, -jnp.inf)
        top = jnp.maximum(own, past).max(axis=1, keepdims=True)
        own, past = jnp.exp(own - top), jnp.exp(past - top)
        total = (own + past).sum(axis=1, keepdims=True)
        inverse = 1.0 / total
        own, past = (own * inverse).astype(BF), (past * inverse).astype(BF)
        part = dot(own, v_ref[0, :, at]) + dot(past, vp_ref[0, :, at])
        part = part.astype(BF)
        att_ref[:, at] = part
        resid = in_ref[0, :, at].astype(F32) + part.astype(F32)
        resid_ref[group, :, at] = resid
        squares = squares + resid * resid

    @pl.when(group == 0)
    def _():
        squares_ref[...] = squares

    @pl.when(group > 0)
    def _():
        squares_ref[...] += squares

    @pl.when(group == groups - 1)
    def _():
        parts = resid_ref.shape[0]
        width = parts * part_width
        inv_rms = lax.rsqrt(squares_ref[...].sum(axis=1, keepdims=True) / width + 1e-06)
        _, _, slot = routing(ids_ref[0, 0:1], ids_ref[0, 1:2], here)
        table = placing_table(slot, slots, len(out_refs))
        for n in range(parts):
            at = slice(n * part_width, (n + 1) * part_width)
            normed = (resid_ref[n] * inv_rms * gain_ref[:, at]).astype(BF)
            packed = dot(table, normed).astype(BF)
            for k, out in enumerate(out_refs):
                out[:, at] = packed[k * slots : (k + 1) * slots]


def quarter(j, size):
    mine = lax.axis_index("fsdp") * lax.axis_size("ctx") + lax.axis_index("ctx")
    return pl.ds(pl.multiple_of((mine ^ j) * size, size), size)


def gather_rows(rows, slots, x):
    for j in range(x.shape[0]):
        at = quarter(j, x.shape[2])
        for k, block in enumerate(rows):
            x[j, k * slots : (k + 1) * slots] = block[:, at]


def summed(terms):
    total = terms[0]
    for term in terms[1:]:
        total = total + term
    return total


def hidden_kernel(count, pieces, *refs):
    rows, gates, refs = refs[:count], refs[count : count + pieces], refs[count + pieces :]
    others, refs = refs[:pieces], refs[pieces:]
    hidden_ref, slope_ref, silu_ref, x = refs
    gather_rows(rows, rows[0].shape[0], x)
    step = 256
    for n in range(hidden_ref.shape[1] // step):
        at = slice(n * step, (n + 1) * step)
        gate_pre = summed([dot(x[j], gate[0, :, at]) for j, gate in enumerate(gates)])
        up_pre = summed([dot(x[j], other[0, :, at]) for j, other in enumerate(others)])
        sig = 1.0 / (1.0 + jnp.exp(-gate_pre))
        silu = gate_pre * sig
        hidden_ref[:, at] = (silu * up_pre).astype(BF)
        slope_ref[:, at] = up_pre * sig * (1.0 + gate_pre * (1.0 - sig))
        silu_ref[:, at] = silu


def out_kernel(pieces, hidden_ref, *refs):
    others, outs = refs[:pieces], refs[pieces:]
    slots = outs[0].shape[0]
    for j, other in enumerate(others):
        part = dot_t(hidden_ref[...], other[1]).astype(BF)
        for k, out in enumerate(outs):
            out[:, quarter(j, other.shape[1])] = part[k * slots : (k + 1) * slots]


def backward_kernel(rows_count, pieces, slots, *refs):
    rows, gates, refs = refs[:rows_count], refs[rows_count : rows_count + pieces], refs[rows_count + pieces :]
    others, slope_ref, silu_ref, refs = refs[:pieces], refs[pieces], refs[pieces + 1], refs[pieces + 2 :]
    outs, (x, gate_grad, up_grad) = refs[:-3], refs[-3:]
    gather_rows(rows, slots, x)
    step = 256
    for n in range(gate_grad.shape[1] // step):
        at = slice(n * step, (n + 1) * step)
        hidden_grad = summed([dot(x[j], other[1, :, at]) for j, other in enumerate(others)])
        gate_grad[:, at] = (hidden_grad * slope_ref[:, at]).astype(BF)
        up_grad[:, at] = (hidden_grad * silu_ref[:, at]).astype(BF)
    for j, (gate, other) in enumerate(zip(gates, others)):
        part = dot_t(gate_grad[...], gate[0]) + dot_t(up_grad[...], other[0])
        part = part.astype(BF)
        for k, out in enumerate(outs):
            out[:, quarter(j, gate.shape[1])] = part[k * slots : (k + 1) * slots]


def mixed(ids_ref, weight_ref, backs, kinds, at, cache):
    if not cache:
        first, second, slot = routing(ids_ref[0, 0:1], ids_ref[0, 1:2], lax.axis_index("expert"))
        slots = backs[0].shape[0]
        gates = [column(weight_ref[0, j : j + 1]) for j in range(2)]
        for k in kinds:
            place = placing(slot, k, slots)[:, :slots].astype(BF)
            weight = jnp.where(first == k, gates[0], 0.0) + jnp.where(second == k, gates[1], 0.0)
            cache.append((place, weight))
    return summed([weight * dot(place, back[:, at]) for back, (place, weight) in zip(backs, cache)])


def layer_kernel(ids_ref, weight_ref, in_ref, att_ref, *refs):
    backs, out_ref = refs[:-1], refs[-1]
    step, cache = 512, []
    for n in range(in_ref.shape[2] // step):
        at = slice(n * step, (n + 1) * step)
        resid = in_ref[0, :, at].astype(F32) + att_ref[:, at].astype(F32)
        out_ref[0, :, at] = (resid + mixed(ids_ref, weight_ref, backs, range(len(backs)), at, cache)).astype(BF)


def near_grad_kernel(ids_ref, weight_ref, in_ref, att_ref, *refs):
    backs, sum_ref, rms_ref, place_ref, share_ref = refs[:-4], refs[-4], refs[-3], refs[-2], refs[-1]
    tok, width = in_ref.shape[1], in_ref.shape[2]
    step, cache = 512, []
    squares = jnp.zeros((tok, 1), F32)
    for n in range(width // step):
        at = slice(n * step, (n + 1) * step)
        resid = in_ref[0, :, at].astype(F32) + att_ref[:, at].astype(F32)
        sum_ref[:, at] = mixed(ids_ref, weight_ref, backs, range(len(backs)), at, cache)
        squares = squares + (resid * resid).sum(axis=1, keepdims=True)
    rms_ref[...] = jnp.broadcast_to(lax.rsqrt(squares / width + 1e-06), rms_ref.shape)
    first, second, slot = routing(ids_ref[0, 0:1], ids_ref[0, 1:2], lax.axis_index("expert"))
    last = len(backs)
    place_ref[...] = placing(slot, last, 0).astype(BF)
    gates = [column(weight_ref[0, j : j + 1]) for j in range(2)]
    share = jnp.where(first == last, gates[0], 0.0) + jnp.where(second == last, gates[1], 0.0)
    share_ref[...] = jnp.broadcast_to(share, share_ref.shape)


def grad_kernel(in_ref, att_ref, gain_ref, up_ref, sum_ref, rms_ref, place_ref, share_ref, back_ref, out_hbm, *refs):
    gained_ref, out_ref, sems = refs
    tok, width = in_ref.shape[1], in_ref.shape[2]
    step = 512
    place, share = place_ref[:, : back_ref.shape[0]], share_ref[:, 0:1]
    cross = jnp.zeros((tok, 1), F32)
    for n in range(width // step):
        at = slice(n * step, (n + 1) * step)
        resid = in_ref[0, :, at].astype(F32) + att_ref[:, at].astype(F32)
        gained = gain_ref[:, at] * (sum_ref[:, at] + share * dot(place, back_ref[:, at]))
        gained_ref[:, at] = gained
        cross = cross + (resid * gained).sum(axis=1, keepdims=True)
    inv_rms = rms_ref[:, 0:1]
    pull = inv_rms * inv_rms * inv_rms * (cross / width)
    copies = []
    for n in range(width // step):
        at = slice(n * step, (n + 1) * step)
        resid = in_ref[0, :, at].astype(F32) + att_ref[:, at].astype(F32)
        out_ref[:, at] = (up_ref[0, :, at].astype(F32) + inv_rms * gained_ref[:, at] - resid * pull).astype(BF)
        copies.append(pltpu.make_async_copy(out_ref.at[:, at], out_hbm.at[0, :, at], sems.at[n]))
        copies[-1].start()
    for copy in copies:
        copy.wait()


def shards(
    inputs, queries, keys, values, doc_ids, norm_gain, expert_ids, gate_weights, w_gate, w_up, w_down, out_grad
):
    tok, width = inputs.shape[1], inputs.shape[2]
    hidden_count = w_gate.shape[2]
    peers = lax.axis_size("expert")
    slots = 5 * tok // (2 * peers)
    slots = -(-slots // 16) * 16
    pieces = lax.axis_size("fsdp") * lax.axis_size("ctx")
    total = peers * slots
    slab = jax.ShapeDtypeStruct((slots, width), BF)
    slabs = [slab] * peers
    gain = norm_gain.reshape(1, width)
    ids, gates = jnp.swapaxes(expert_ids, 1, 2), jnp.swapaxes(gate_weights, 1, 2)


    def call(kernel, name, out_shape, count, scratch=(), mib=24):
        return pl.pallas_call(
            kernel,
            out_shape=out_shape,
            in_specs=[VM] * count,
            out_specs=[VM] * len(out_shape) if isinstance(out_shape, list) else VM,
            scratch_shapes=list(scratch),
            compiler_params=params(mib),
            name=name,
        )

    def exchanged(blocks):
        return [block if k == 0 else swapped(block, "expert", k) for k, block in enumerate(blocks)]

    def over_core(block):
        return swapped(block, "ctx", 1)

    def over_x(block):
        return [swapped(block, "fsdp", dx) for dx in range(1, lax.axis_size("fsdp"))]

    both = jnp.concatenate([keys, values], 2)
    previous = shifted(both, ("expert", "ctx"), 1)
    own_others = pl.pallas_call(
        prepare_kernel,
        out_shape=jax.ShapeDtypeStruct((2, w_gate.shape[1], hidden_count), BF),
        in_specs=[pl.BlockSpec(memory_space=pl.ANY)] * 2,
        out_specs=pl.BlockSpec(memory_space=pl.ANY),
        scratch_shapes=[
            pltpu.VMEM((2, w_gate.shape[1], hidden_count), BF),
            pltpu.VMEM(w_down.shape[1:], BF),
            pltpu.SemaphoreType.DMA((4,)),
        ],
        compiler_params=params(56),
        name="prepare",
    )(w_up, after(w_down, both))
    sent_grads = call(lambda *refs: pack_kernel(slots, *refs), "pack_grad", slabs, 2)(ids, after(out_grad, own_others))
    grads = [
        block if k < 2 else swapped(after(block, previous), "expert", k) for k, block in enumerate(sent_grads[:-1])
    ]
    gates_x, others_x = over_x(w_gate), over_x(own_others)

    parts = 4
    cut = width // parts

    def by_part(*dims):
        return pl.BlockSpec((*dims, cut), lambda n: (0,) * len(dims) + (n,))

    def fixed(*dims):
        return pl.BlockSpec(dims, lambda n: (0,) * len(dims))

    attended, *sent_rows = pl.pallas_call(
        lambda *refs: attend_kernel(slots, *refs),
        out_shape=[jax.ShapeDtypeStruct((tok, width), BF)] + slabs,
        grid=(parts,),
        in_specs=[by_part(1, tok)] * 3
        + [by_part(1, tok), pl.BlockSpec((1, tok, cut), lambda n: (0, 0, n + parts)), fixed(*doc_ids.shape), by_part(1, tok), fixed(1, width), fixed(*ids.shape)],
        out_specs=[by_part(tok)] + [fixed(slots, width)] * peers,
        scratch_shapes=[pltpu.VMEM((parts, tok, cut), F32), pltpu.VMEM((tok, HD), F32)],
        compiler_params=params(16),
        name="attend",
    )(queries, keys, values, previous, previous, doc_ids, inputs, gain, ids)
    rows = exchanged([after(block, grads[-1]) if k != peers - 1 else block for k, block in enumerate(sent_rows)])

    all_gates, all_others = [w_gate, over_core(after(w_gate, attended))], [own_others, over_core(after(own_others, attended))]
    for gate, other in zip(gates_x, others_x):
        all_gates += [gate, over_core(after(gate, *rows[1:]))]
        all_others += [other, over_core(after(other, *rows[1:]))]
    grads.append(swapped(after(sent_grads[-1], rows[1]), "expert", peers - 1))

    wide = jax.ShapeDtypeStruct((total, hidden_count), F32)
    x_scratch = pltpu.VMEM((pieces, total, w_gate.shape[1]), BF)
    hidden, slope, silu = call(
        lambda *refs: hidden_kernel(peers, pieces, *refs),
        "hidden",
        [jax.ShapeDtypeStruct((total, hidden_count), BF), wide, wide],
        peers + 2 * pieces,
        [x_scratch],
    )(*rows, *all_gates, *all_others)
    grads[1] = swapped(after(grads[1], hidden), "expert", 1)
    served_out = call(lambda *refs: out_kernel(pieces, *refs), "served", slabs, 1 + pieces)(hidden, *all_others)
    back_out = exchanged(served_out)

    served_grad = call(
        lambda *refs: backward_kernel(len(grads), pieces, slots, *refs),
        "backward",
        slabs,
        len(grads) + 2 * pieces + 2,
        [x_scratch] + [pltpu.VMEM((total, hidden_count), BF)] * 2,
    )(*grads, *all_gates, *all_others, slope, silu)
    back_grad = exchanged(served_grad)

    out_block = jax.ShapeDtypeStruct(inputs.shape, BF)
    layer_out = pl.pallas_call(
        layer_kernel,
        out_shape=out_block,
        in_specs=[VM] * (4 + peers),
        out_specs=VM,
        compiler_params=params(32),
        name="layer",
    )(ids, gates, inputs, attended, *back_out)
    flat = jax.ShapeDtypeStruct((tok, 128), F32)
    near_sum, inv_rms, place, share = call(
        near_grad_kernel,
        "near_grad",
        [jax.ShapeDtypeStruct((tok, width), F32), flat, jax.ShapeDtypeStruct((tok, 128), BF), flat],
        3 + peers,
    )(ids, gates, inputs, after(attended, layer_out), *back_grad[:-1])
    input_grad = pl.pallas_call(
        grad_kernel,
        out_shape=out_block,
        in_specs=[VM] * 9,
        out_specs=pl.BlockSpec(memory_space=pl.ANY),
        scratch_shapes=[
            pltpu.VMEM((tok, width), F32),
            pltpu.VMEM((tok, width), BF),
            pltpu.SemaphoreType.DMA((width // 512,)),
        ],
        compiler_params=params(16),
        name="grad",
    )(inputs, attended, gain, out_grad, near_sum, inv_rms, place, share, back_grad[-1])
    return layer_out, input_grad


def solution(mesh):
    rows = P(("groups", "fsdp"), ("expert", "ctx"), None)
    in_specs = (
        rows,
        rows,
        rows,
        rows,
        P(("groups", "fsdp"), None),
        P(),
        rows,
        rows,
        P("expert", ("fsdp", "ctx"), None),
        P("expert", ("fsdp", "ctx"), None),
        P("expert", None, ("fsdp", "ctx")),
        rows,
    )
    return jax.shard_map(shards, mesh=mesh, in_specs=in_specs, out_specs=(rows, rows), check_vma=False)
```

```python
import jax
import jax.numpy as jnp
from jax import lax
from jax.experimental import pallas as pl
from jax.experimental.pallas import tpu as pltpu
from jax.sharding import PartitionSpec as P

HEADS = 16
HD = 128
BF = jnp.bfloat16
F32 = jnp.float32
VM = pl.BlockSpec(memory_space=pltpu.VMEM)
MIB = 1024 * 1024


def params(mib):
    return pltpu.CompilerParams(vmem_limit_bytes=mib * MIB)


def swapped(block, axis, distance):
    count = lax.axis_size(axis)
    return lax.ppermute(block, axis, [(i, i ^ distance) for i in range(count)])


def shifted(block, axis, distance):
    devices = range(lax.axis_size(axis))
    route = [(i - distance, i) for i in devices if i - distance in devices]
    return lax.ppermute(block, axis, route)


def after(block, *others):
    return lax.optimization_barrier((block, *others))[0]


def dot(a, b):
    return jnp.dot(a, b, preferred_element_type=F32)


def dot_t(a, b):
    return lax.dot_general(a, b, (((1,), (1,)), ((), ())), preferred_element_type=F32)


def column(row):
    tok = row.shape[1]
    return jnp.broadcast_to(row, (tok, tok)).T[:, 0:1]


def routing(first, second, here):
    tok = first.shape[1]
    lane = lax.broadcasted_iota(jnp.int32, (tok, 128), 1)
    row = lax.broadcasted_iota(jnp.int32, (tok, tok), 0)
    col = lax.broadcasted_iota(jnp.int32, (tok, tok), 1)
    first, second = column(first) ^ here, column(second) ^ here
    chosen = (first == lane) | (second == lane)
    before = (col < row).astype(BF)
    rank = dot(before, chosen.astype(BF))
    slot = jnp.where(chosen, rank, -1.0)
    return first, second, slot


def placing(slot, k, slots):
    tok = slot.shape[0]
    lane = lax.broadcasted_iota(jnp.int32, (tok, 128), 1)
    return jnp.where(lane == slot[:, k : k + 1].astype(jnp.int32), 1.0, 0.0)


def placing_table(slot, slots, count):
    return jnp.concatenate([placing(slot, k, slots).T[:slots] for k in range(count)], 0).astype(BF)


def pack(rows, slot, slots, out_refs):
    packed = dot(placing_table(slot, slots, len(out_refs)), rows).astype(BF)
    for k, out in enumerate(out_refs):
        out[...] = packed[k * slots : (k + 1) * slots]


def prepare_kernel(u_hbm, d_hbm, weight_hbm, weight, down, sems):
    pairs = [
        (d_hbm.at[0], down),
        (u_hbm.at[0], weight.at[0]),
        (weight.at[0], weight_hbm.at[0]),
        (weight.at[1], weight_hbm.at[1]),
    ]
    copies = [pltpu.make_async_copy(source, target, sems.at[n]) for n, (source, target) in enumerate(pairs)]
    copies[0].start()
    copies[1].start()
    copies[1].wait()
    copies[2].start()
    copies[0].wait()
    weight[1] = down[...].T
    copies[3].start()
    copies[2].wait()
    copies[3].wait()


def pack_kernel(slots, ids_ref, rows_ref, *out_refs):
    _, _, slot = routing(ids_ref[0, 0:1], ids_ref[0, 1:2], lax.axis_index("expert"))
    pack(rows_ref[0], slot, slots, out_refs)


def attend_kernel(
    slots, q_ref, k_ref, v_ref, kp_ref, vp_ref, doc_ref, in_ref, gain_ref, ids_ref, att_ref, *refs
):
    out_refs, (resid_ref, squares_ref) = refs[:-2], refs[-2:]
    group, groups = pl.program_id(0), pl.num_programs(0)
    tok, part_width = q_ref.shape[1], q_ref.shape[2]
    here = lax.axis_index("expert")
    first = (here * lax.axis_size("ctx") + lax.axis_index("ctx")) * tok
    before = jnp.maximum(first - tok, 0)
    own_docs = doc_ref[:, pl.ds(pl.multiple_of(first, tok), tok)]
    past_docs = doc_ref[:, pl.ds(pl.multiple_of(before, tok), tok)]
    row = lax.broadcasted_iota(jnp.int32, (tok, tok), 0)
    col = lax.broadcasted_iota(jnp.int32, (tok, tok), 1)
    own_all = jnp.broadcast_to(own_docs, (tok, tok))
    query_docs = own_all.T
    see_own = (query_docs == own_all) & (col <= row)
    see_past = (query_docs == past_docs) & (first > 0)
    scale = HD ** (-0.5)
    squares = jnp.zeros((tok, HD), F32)
    for h in range(part_width // HD):
        at = slice(h * HD, (h + 1) * HD)
        q = q_ref[0, :, at]
        own = jnp.where(see_own, dot_t(q, k_ref[0, :, at]) * scale, -jnp.inf)
        past = jnp.where(see_past, dot_t(q, kp_ref[0, :, at]) * scale, -jnp.inf)
        top = jnp.maximum(own, past).max(axis=1, keepdims=True)
        own, past = jnp.exp(own - top), jnp.exp(past - top)
        total = (own + past).sum(axis=1, keepdims=True)
        inverse = 1.0 / total
        own, past = (own * inverse).astype(BF), (past * inverse).astype(BF)
        part = dot(own, v_ref[0, :, at]) + dot(past, vp_ref[0, :, at])
        part = part.astype(BF)
        att_ref[:, at] = part
        resid = in_ref[0, :, at].astype(F32) + part.astype(F32)
        resid_ref[group, :, at] = resid
        squares = squares + resid * resid

    @pl.when(group == 0)
    def _():
        squares_ref[...] = squares

    @pl.when(group > 0)
    def _():
        squares_ref[...] += squares

    @pl.when(group == groups - 1)
    def _():
        parts = resid_ref.shape[0]
        width = parts * part_width
        inv_rms = lax.rsqrt(squares_ref[...].sum(axis=1, keepdims=True) / width + 1e-06)
        _, _, slot = routing(ids_ref[0, 0:1], ids_ref[0, 1:2], here)
        table = placing_table(slot, slots, len(out_refs))
        for n in range(parts):
            at = slice(n * part_width, (n + 1) * part_width)
            normed = (resid_ref[n] * inv_rms * gain_ref[:, at]).astype(BF)
            packed = dot(table, normed).astype(BF)
            for k, out in enumerate(out_refs):
                out[:, at] = packed[k * slots : (k + 1) * slots]


def quarter(j, size):
    mine = lax.axis_index("fsdp") * lax.axis_size("ctx") + lax.axis_index("ctx")
    return pl.ds(pl.multiple_of((mine ^ j) * size, size), size)


def gather_rows(rows, slots, x):
    for j in range(x.shape[0]):
        at = quarter(j, x.shape[2])
        for k, block in enumerate(rows):
            x[j, k * slots : (k + 1) * slots] = block[:, at]


def summed(terms):
    total = terms[0]
    for term in terms[1:]:
        total = total + term
    return total


def hidden_kernel(count, pieces, *refs):
    rows, gates, refs = refs[:count], refs[count : count + pieces], refs[count + pieces :]
    others, refs = refs[:pieces], refs[pieces:]
    hidden_ref, slope_ref, silu_ref, x = refs
    gather_rows(rows, rows[0].shape[0], x)
    step = 256
    for n in range(hidden_ref.shape[1] // step):
        at = slice(n * step, (n + 1) * step)
        gate_pre = summed([dot(x[j], gate[0, :, at]) for j, gate in enumerate(gates)])
        up_pre = summed([dot(x[j], other[0, :, at]) for j, other in enumerate(others)])
        sig = 1.0 / (1.0 + jnp.exp(-gate_pre))
        silu = gate_pre * sig
        hidden_ref[:, at] = (silu * up_pre).astype(BF)
        slope_ref[:, at] = up_pre * sig * (1.0 + gate_pre * (1.0 - sig))
        silu_ref[:, at] = silu


def out_kernel(pieces, hidden_ref, *refs):
    others, outs = refs[:pieces], refs[pieces:]
    slots = outs[0].shape[0]
    for j, other in enumerate(others):
        part = dot_t(hidden_ref[...], other[1]).astype(BF)
        for k, out in enumerate(outs):
            out[:, quarter(j, other.shape[1])] = part[k * slots : (k + 1) * slots]


def backward_kernel(rows_count, pieces, slots, *refs):
    rows, gates, refs = refs[:rows_count], refs[rows_count : rows_count + pieces], refs[rows_count + pieces :]
    others, slope_ref, silu_ref, refs = refs[:pieces], refs[pieces], refs[pieces + 1], refs[pieces + 2 :]
    outs, (x, gate_grad, up_grad) = refs[:-3], refs[-3:]
    gather_rows(rows, slots, x)
    step = 256
    for n in range(gate_grad.shape[1] // step):
        at = slice(n * step, (n + 1) * step)
        hidden_grad = summed([dot(x[j], other[1, :, at]) for j, other in enumerate(others)])
        gate_grad[:, at] = (hidden_grad * slope_ref[:, at]).astype(BF)
        up_grad[:, at] = (hidden_grad * silu_ref[:, at]).astype(BF)
    for j, (gate, other) in enumerate(zip(gates, others)):
        part = dot_t(gate_grad[...], gate[0]) + dot_t(up_grad[...], other[0])
        part = part.astype(BF)
        for k, out in enumerate(outs):
            out[:, quarter(j, gate.shape[1])] = part[k * slots : (k + 1) * slots]


def mixed(ids_ref, weight_ref, backs, kinds, at, cache):
    if not cache:
        first, second, slot = routing(ids_ref[0, 0:1], ids_ref[0, 1:2], lax.axis_index("expert"))
        slots = backs[0].shape[0]
        gates = [column(weight_ref[0, j : j + 1]) for j in range(2)]
        for k in kinds:
            place = placing(slot, k, slots)[:, :slots].astype(BF)
            weight = jnp.where(first == k, gates[0], 0.0) + jnp.where(second == k, gates[1], 0.0)
            cache.append((place, weight))
    return summed([weight * dot(place, back[:, at]) for back, (place, weight) in zip(backs, cache)])


def layer_kernel(ids_ref, weight_ref, in_ref, att_ref, *refs):
    backs, out_ref = refs[:-1], refs[-1]
    step, cache = 512, []
    for n in range(in_ref.shape[2] // step):
        at = slice(n * step, (n + 1) * step)
        resid = in_ref[0, :, at].astype(F32) + att_ref[:, at].astype(F32)
        out_ref[0, :, at] = (resid + mixed(ids_ref, weight_ref, backs, range(len(backs)), at, cache)).astype(BF)


def near_grad_kernel(ids_ref, weight_ref, in_ref, att_ref, *refs):
    backs, sum_ref, rms_ref, place_ref, share_ref = refs[:-4], refs[-4], refs[-3], refs[-2], refs[-1]
    tok, width = in_ref.shape[1], in_ref.shape[2]
    step, cache = 512, []
    squares = jnp.zeros((tok, 1), F32)
    for n in range(width // step):
        at = slice(n * step, (n + 1) * step)
        resid = in_ref[0, :, at].astype(F32) + att_ref[:, at].astype(F32)
        sum_ref[:, at] = mixed(ids_ref, weight_ref, backs, range(len(backs)), at, cache)
        squares = squares + (resid * resid).sum(axis=1, keepdims=True)
    rms_ref[...] = jnp.broadcast_to(lax.rsqrt(squares / width + 1e-06), rms_ref.shape)
    first, second, slot = routing(ids_ref[0, 0:1], ids_ref[0, 1:2], lax.axis_index("expert"))
    last = len(backs)
    place_ref[...] = placing(slot, last, 0).astype(BF)
    gates = [column(weight_ref[0, j : j + 1]) for j in range(2)]
    share = jnp.where(first == last, gates[0], 0.0) + jnp.where(second == last, gates[1], 0.0)
    share_ref[...] = jnp.broadcast_to(share, share_ref.shape)


def grad_kernel(in_ref, att_ref, gain_ref, up_ref, sum_ref, rms_ref, place_ref, share_ref, back_ref, out_hbm, *refs):
    gained_ref, out_ref, sems = refs
    tok, width = in_ref.shape[1], in_ref.shape[2]
    step = 512
    place, share = place_ref[:, : back_ref.shape[0]], share_ref[:, 0:1]
    cross = jnp.zeros((tok, 1), F32)
    for n in range(width // step):
        at = slice(n * step, (n + 1) * step)
        resid = in_ref[0, :, at].astype(F32) + att_ref[:, at].astype(F32)
        gained = gain_ref[:, at] * (sum_ref[:, at] + share * dot(place, back_ref[:, at]))
        gained_ref[:, at] = gained
        cross = cross + (resid * gained).sum(axis=1, keepdims=True)
    inv_rms = rms_ref[:, 0:1]
    pull = inv_rms * inv_rms * inv_rms * (cross / width)
    copies = []
    for n in range(width // step):
        at = slice(n * step, (n + 1) * step)
        resid = in_ref[0, :, at].astype(F32) + att_ref[:, at].astype(F32)
        out_ref[:, at] = (up_ref[0, :, at].astype(F32) + inv_rms * gained_ref[:, at] - resid * pull).astype(BF)
        copies.append(pltpu.make_async_copy(out_ref.at[:, at], out_hbm.at[0, :, at], sems.at[n]))
        copies[-1].start()
    for copy in copies:
        copy.wait()


def shards(
    inputs, queries, keys, values, doc_ids, norm_gain, expert_ids, gate_weights, w_gate, w_up, w_down, out_grad
):
    tok, width = inputs.shape[1], inputs.shape[2]
    hidden_count = w_gate.shape[2]
    peers = lax.axis_size("expert")
    slots = 5 * tok // (2 * peers)
    slots = -(-slots // 16) * 16
    pieces = lax.axis_size("fsdp") * lax.axis_size("ctx")
    total = peers * slots
    slab = jax.ShapeDtypeStruct((slots, width), BF)
    slabs = [slab] * peers
    gain = norm_gain.reshape(1, width)
    ids, gates = jnp.swapaxes(expert_ids, 1, 2), jnp.swapaxes(gate_weights, 1, 2)


    def call(kernel, name, out_shape, count, scratch=(), mib=24):
        return pl.pallas_call(
            kernel,
            out_shape=out_shape,
            in_specs=[VM] * count,
            out_specs=[VM] * len(out_shape) if isinstance(out_shape, list) else VM,
            scratch_shapes=list(scratch),
            compiler_params=params(mib),
            name=name,
        )

    def exchanged(blocks):
        return [block if k == 0 else swapped(block, "expert", k) for k, block in enumerate(blocks)]

    def over_core(block):
        return swapped(block, "ctx", 1)

    def over_x(block):
        return [swapped(block, "fsdp", dx) for dx in range(1, lax.axis_size("fsdp"))]

    both = jnp.pad(keys, ((0, 0), (0, 0), (0, width))) + jnp.pad(values, ((0, 0), (0, 0), (width, 0)))
    previous = shifted(both, ("expert", "ctx"), 1)
    own_others = pl.pallas_call(
        prepare_kernel,
        out_shape=jax.ShapeDtypeStruct((2, w_gate.shape[1], hidden_count), BF),
        in_specs=[pl.BlockSpec(memory_space=pl.ANY)] * 2,
        out_specs=pl.BlockSpec(memory_space=pl.ANY),
        scratch_shapes=[
            pltpu.VMEM((2, w_gate.shape[1], hidden_count), BF),
            pltpu.VMEM(w_down.shape[1:], BF),
            pltpu.SemaphoreType.DMA((4,)),
        ],
        compiler_params=params(56),
        name="prepare",
    )(w_up, after(w_down, both))
    sent_grads = call(lambda *refs: pack_kernel(slots, *refs), "pack_grad", slabs, 2)(ids, after(out_grad, own_others))
    grads = [
        block if k < 2 else swapped(after(block, previous), "expert", k) for k, block in enumerate(sent_grads[:-1])
    ]
    gates_x, others_x = over_x(w_gate), over_x(own_others)

    parts = 4
    cut = width // parts

    def by_part(*dims):
        return pl.BlockSpec((*dims, cut), lambda n: (0,) * len(dims) + (n,))

    def fixed(*dims):
        return pl.BlockSpec(dims, lambda n: (0,) * len(dims))

    attended, *sent_rows = pl.pallas_call(
        lambda *refs: attend_kernel(slots, *refs),
        out_shape=[jax.ShapeDtypeStruct((tok, width), BF)] + slabs,
        grid=(parts,),
        in_specs=[by_part(1, tok)] * 3
        + [by_part(1, tok), pl.BlockSpec((1, tok, cut), lambda n: (0, 0, n + parts)), fixed(*doc_ids.shape), by_part(1, tok), fixed(1, width), fixed(*ids.shape)],
        out_specs=[by_part(tok)] + [fixed(slots, width)] * peers,
        scratch_shapes=[pltpu.VMEM((parts, tok, cut), F32), pltpu.VMEM((tok, HD), F32)],
        compiler_params=params(16),
        name="attend",
    )(queries, keys, values, previous, previous, doc_ids, inputs, gain, ids)
    rows = exchanged([after(block, grads[-1]) if k != peers - 1 else block for k, block in enumerate(sent_rows)])

    all_gates, all_others = [w_gate, over_core(after(w_gate, attended))], [own_others, over_core(after(own_others, attended))]
    for gate, other in zip(gates_x, others_x):
        all_gates += [gate, over_core(after(gate, *rows[1:]))]
        all_others += [other, over_core(after(other, *rows[1:]))]
    grads.append(swapped(after(sent_grads[-1], rows[1]), "expert", peers - 1))

    wide = jax.ShapeDtypeStruct((total, hidden_count), F32)
    x_scratch = pltpu.VMEM((pieces, total, w_gate.shape[1]), BF)
    hidden, slope, silu = call(
        lambda *refs: hidden_kernel(peers, pieces, *refs),
        "hidden",
        [jax.ShapeDtypeStruct((total, hidden_count), BF), wide, wide],
        peers + 2 * pieces,
        [x_scratch],
    )(*rows, *all_gates, *all_others)
    grads[1] = swapped(after(grads[1], hidden), "expert", 1)
    served_out = call(lambda *refs: out_kernel(pieces, *refs), "served", slabs, 1 + pieces)(hidden, *all_others)
    back_out = exchanged(served_out)

    served_grad = call(
        lambda *refs: backward_kernel(len(grads), pieces, slots, *refs),
        "backward",
        slabs,
        len(grads) + 2 * pieces + 2,
        [x_scratch] + [pltpu.VMEM((total, hidden_count), BF)] * 2,
    )(*grads, *all_gates, *all_others, slope, silu)
    back_grad = exchanged(served_grad)

    out_block = jax.ShapeDtypeStruct(inputs.shape, BF)
    layer_out = pl.pallas_call(
        layer_kernel,
        out_shape=out_block,
        in_specs=[VM] * (4 + peers),
        out_specs=VM,
        compiler_params=params(32),
        name="layer",
    )(ids, gates, inputs, attended, *back_out)
    flat = jax.ShapeDtypeStruct((tok, 128), F32)
    near_sum, inv_rms, place, share = call(
        near_grad_kernel,
        "near_grad",
        [jax.ShapeDtypeStruct((tok, width), F32), flat, jax.ShapeDtypeStruct((tok, 128), BF), flat],
        3 + peers,
    )(ids, gates, inputs, after(attended, layer_out), *back_grad[:-1])
    input_grad = pl.pallas_call(
        grad_kernel,
        out_shape=out_block,
        in_specs=[VM] * 9,
        out_specs=pl.BlockSpec(memory_space=pl.ANY),
        scratch_shapes=[
            pltpu.VMEM((tok, width), F32),
            pltpu.VMEM((tok, width), BF),
            pltpu.SemaphoreType.DMA((width // 512,)),
        ],
        compiler_params=params(16),
        name="grad",
    )(inputs, attended, gain, out_grad, near_sum, inv_rms, place, share, back_grad[-1])
    return layer_out, input_grad


def solution(mesh):
    rows = P(("groups", "fsdp"), ("expert", "ctx"), None)
    in_specs = (
        rows,
        rows,
        rows,
        rows,
        P(("groups", "fsdp"), None),
        P(),
        rows,
        rows,
        P("expert", ("fsdp", "ctx"), None),
        P("expert", ("fsdp", "ctx"), None),
        P("expert", None, ("fsdp", "ctx")),
        rows,
    )
    return jax.shard_map(shards, mesh=mesh, in_specs=in_specs, out_specs=(rows, rows), check_vma=False)
```

```python
import jax
import jax.numpy as jnp
from jax import lax
from jax.experimental import pallas as pl
from jax.experimental.pallas import tpu as pltpu
from jax.sharding import PartitionSpec as P

HEADS = 16
HD = 128
BF = jnp.bfloat16
F32 = jnp.float32
VM = pl.BlockSpec(memory_space=pltpu.VMEM)
MIB = 1024 * 1024


def params(mib):
    return pltpu.CompilerParams(vmem_limit_bytes=mib * MIB)


def swapped(block, axis, distance):
    count = lax.axis_size(axis)
    return lax.ppermute(block, axis, [(i, i ^ distance) for i in range(count)])


def shifted(block, axis, distance):
    devices = range(lax.axis_size(axis))
    route = [(i - distance, i) for i in devices if i - distance in devices]
    return lax.ppermute(block, axis, route)


def after(block, *others):
    return lax.optimization_barrier((block, *others))[0]


def dot(a, b):
    return jnp.dot(a, b, preferred_element_type=F32)


def dot_t(a, b):
    return lax.dot_general(a, b, (((1,), (1,)), ((), ())), preferred_element_type=F32)


def column(row):
    tok = row.shape[1]
    return jnp.broadcast_to(row, (tok, tok)).T[:, 0:1]


def routing(first, second, here):
    tok = first.shape[1]
    lane = lax.broadcasted_iota(jnp.int32, (tok, 128), 1)
    row = lax.broadcasted_iota(jnp.int32, (tok, tok), 0)
    col = lax.broadcasted_iota(jnp.int32, (tok, tok), 1)
    first, second = column(first) ^ here, column(second) ^ here
    chosen = (first == lane) | (second == lane)
    before = (col < row).astype(BF)
    rank = dot(before, chosen.astype(BF))
    slot = jnp.where(chosen, rank, -1.0)
    return first, second, slot


def placing(slot, k, slots):
    tok = slot.shape[0]
    lane = lax.broadcasted_iota(jnp.int32, (tok, 128), 1)
    return jnp.where(lane == slot[:, k : k + 1].astype(jnp.int32), 1.0, 0.0)


def placing_table(slot, slots, count):
    return jnp.concatenate([placing(slot, k, slots).T[:slots] for k in range(count)], 0).astype(BF)


def pack(rows, slot, slots, out_refs):
    packed = dot(placing_table(slot, slots, len(out_refs)), rows).astype(BF)
    for k, out in enumerate(out_refs):
        out[...] = packed[k * slots : (k + 1) * slots]


def prepare_kernel(u_hbm, d_hbm, weight_hbm, weight, down, sems):
    pairs = [
        (d_hbm.at[0], down),
        (u_hbm.at[0], weight.at[0]),
        (weight.at[0], weight_hbm.at[0]),
        (weight.at[1], weight_hbm.at[1]),
    ]
    copies = [pltpu.make_async_copy(source, target, sems.at[n]) for n, (source, target) in enumerate(pairs)]
    copies[0].start()
    copies[1].start()
    copies[1].wait()
    copies[2].start()
    copies[0].wait()
    weight[1] = down[...].T
    copies[3].start()
    copies[2].wait()
    copies[3].wait()


def pack_kernel(slots, ids_ref, rows_ref, *out_refs):
    _, _, slot = routing(ids_ref[0, 0:1], ids_ref[0, 1:2], lax.axis_index("expert"))
    pack(rows_ref[0], slot, slots, out_refs)


def attend_kernel(
    slots, q_ref, k_ref, v_ref, kp_ref, vp_ref, doc_ref, in_ref, gain_ref, ids_ref, att_ref, *refs
):
    out_refs, (resid_ref, squares_ref) = refs[:-2], refs[-2:]
    group, groups = pl.program_id(0), pl.num_programs(0)
    tok, part_width = q_ref.shape[1], q_ref.shape[2]
    here = lax.axis_index("expert")
    first = (here * lax.axis_size("ctx") + lax.axis_index("ctx")) * tok
    before = jnp.maximum(first - tok, 0)
    own_docs = doc_ref[:, pl.ds(pl.multiple_of(first, tok), tok)]
    past_docs = doc_ref[:, pl.ds(pl.multiple_of(before, tok), tok)]
    row = lax.broadcasted_iota(jnp.int32, (tok, tok), 0)
    col = lax.broadcasted_iota(jnp.int32, (tok, tok), 1)
    own_all = jnp.broadcast_to(own_docs, (tok, tok))
    query_docs = own_all.T
    see_own = (query_docs == own_all) & (col <= row)
    see_past = (query_docs == past_docs) & (first > 0)
    scale = HD ** (-0.5)
    squares = jnp.zeros((tok, HD), F32)
    for h in range(part_width // HD):
        at = slice(h * HD, (h + 1) * HD)
        q = q_ref[0, :, at]
        own = jnp.where(see_own, dot_t(q, k_ref[0, :, at]) * scale, -jnp.inf)
        past = jnp.where(see_past, dot_t(q, kp_ref[0, :, at]) * scale, -jnp.inf)
        top = jnp.maximum(own, past).max(axis=1, keepdims=True)
        own, past = jnp.exp(own - top), jnp.exp(past - top)
        total = (own + past).sum(axis=1, keepdims=True)
        inverse = 1.0 / total
        own, past = (own * inverse).astype(BF), (past * inverse).astype(BF)
        part = dot(own, v_ref[0, :, at]) + dot(past, vp_ref[0, :, at])
        part = part.astype(BF)
        att_ref[:, at] = part
        resid = in_ref[0, :, at].astype(F32) + part.astype(F32)
        resid_ref[group, :, at] = resid
        squares = squares + resid * resid

    @pl.when(group == 0)
    def _():
        squares_ref[...] = squares

    @pl.when(group > 0)
    def _():
        squares_ref[...] += squares

    @pl.when(group == groups - 1)
    def _():
        parts = resid_ref.shape[0]
        width = parts * part_width
        inv_rms = lax.rsqrt(squares_ref[...].sum(axis=1, keepdims=True) / width + 1e-06)
        _, _, slot = routing(ids_ref[0, 0:1], ids_ref[0, 1:2], here)
        table = placing_table(slot, slots, len(out_refs))
        for n in range(parts):
            at = slice(n * part_width, (n + 1) * part_width)
            normed = (resid_ref[n] * inv_rms * gain_ref[:, at]).astype(BF)
            packed = dot(table, normed).astype(BF)
            for k, out in enumerate(out_refs):
                out[:, at] = packed[k * slots : (k + 1) * slots]


def quarter(j, size):
    mine = lax.axis_index("fsdp") * lax.axis_size("ctx") + lax.axis_index("ctx")
    return pl.ds(pl.multiple_of((mine ^ j) * size, size), size)


def gather_rows(rows, slots, x):
    for j in range(x.shape[0]):
        at = quarter(j, x.shape[2])
        for k, block in enumerate(rows):
            x[j, k * slots : (k + 1) * slots] = block[:, at]


def summed(terms):
    total = terms[0]
    for term in terms[1:]:
        total = total + term
    return total


def hidden_kernel(count, pieces, *refs):
    rows, gates, refs = refs[:count], refs[count : count + pieces], refs[count + pieces :]
    others, refs = refs[:pieces], refs[pieces:]
    hidden_ref, slope_ref, silu_ref, x = refs
    gather_rows(rows, rows[0].shape[0], x)
    step = 256
    for n in range(hidden_ref.shape[1] // step):
        at = slice(n * step, (n + 1) * step)
        gate_pre = summed([dot(x[j], gate[0, :, at]) for j, gate in enumerate(gates)])
        up_pre = summed([dot(x[j], other[0, :, at]) for j, other in enumerate(others)])
        sig = 1.0 / (1.0 + jnp.exp(-gate_pre))
        silu = gate_pre * sig
        hidden_ref[:, at] = (silu * up_pre).astype(BF)
        slope_ref[:, at] = up_pre * sig * (1.0 + gate_pre * (1.0 - sig))
        silu_ref[:, at] = silu


def out_kernel(pieces, hidden_ref, *refs):
    others, outs = refs[:pieces], refs[pieces:]
    slots = outs[0].shape[0]
    for j, other in enumerate(others):
        part = dot_t(hidden_ref[...], other[1]).astype(BF)
        for k, out in enumerate(outs):
            out[:, quarter(j, other.shape[1])] = part[k * slots : (k + 1) * slots]


def backward_kernel(rows_count, pieces, slots, *refs):
    rows, gates, refs = refs[:rows_count], refs[rows_count : rows_count + pieces], refs[rows_count + pieces :]
    others, slope_ref, silu_ref, refs = refs[:pieces], refs[pieces], refs[pieces + 1], refs[pieces + 2 :]
    outs, (x, gate_grad, up_grad) = refs[:-3], refs[-3:]
    gather_rows(rows, slots, x)
    step = 256
    for n in range(gate_grad.shape[1] // step):
        at = slice(n * step, (n + 1) * step)
        hidden_grad = summed([dot(x[j], other[1, :, at]) for j, other in enumerate(others)])
        gate_grad[:, at] = (hidden_grad * slope_ref[:, at]).astype(BF)
        up_grad[:, at] = (hidden_grad * silu_ref[:, at]).astype(BF)
    for j, (gate, other) in enumerate(zip(gates, others)):
        part = dot_t(gate_grad[...], gate[0]) + dot_t(up_grad[...], other[0])
        part = part.astype(BF)
        for k, out in enumerate(outs):
            out[:, quarter(j, gate.shape[1])] = part[k * slots : (k + 1) * slots]


def mixed(ids_ref, weight_ref, backs, kinds, at, cache):
    if not cache:
        first, second, slot = routing(ids_ref[0, 0:1], ids_ref[0, 1:2], lax.axis_index("expert"))
        slots = backs[0].shape[0]
        gates = [column(weight_ref[0, j : j + 1]) for j in range(2)]
        for k in kinds:
            place = placing(slot, k, slots)[:, :slots].astype(BF)
            weight = jnp.where(first == k, gates[0], 0.0) + jnp.where(second == k, gates[1], 0.0)
            cache.append((place, weight))
    return summed([weight * dot(place, back[:, at]) for back, (place, weight) in zip(backs, cache)])


def layer_kernel(ids_ref, weight_ref, in_ref, att_ref, *refs):
    backs, out_ref = refs[:-1], refs[-1]
    step, cache = 512, []
    for n in range(in_ref.shape[2] // step):
        at = slice(n * step, (n + 1) * step)
        resid = in_ref[0, :, at].astype(F32) + att_ref[:, at].astype(F32)
        out_ref[0, :, at] = (resid + mixed(ids_ref, weight_ref, backs, range(len(backs)), at, cache)).astype(BF)


def near_grad_kernel(ids_ref, weight_ref, in_ref, att_ref, *refs):
    backs, sum_ref, rms_ref, place_ref, share_ref = refs[:-4], refs[-4], refs[-3], refs[-2], refs[-1]
    tok, width = in_ref.shape[1], in_ref.shape[2]
    step, cache = 512, []
    squares = jnp.zeros((tok, 1), F32)
    for n in range(width // step):
        at = slice(n * step, (n + 1) * step)
        resid = in_ref[0, :, at].astype(F32) + att_ref[:, at].astype(F32)
        sum_ref[:, at] = mixed(ids_ref, weight_ref, backs, range(len(backs)), at, cache)
        squares = squares + (resid * resid).sum(axis=1, keepdims=True)
    rms_ref[...] = jnp.broadcast_to(lax.rsqrt(squares / width + 1e-06), rms_ref.shape)
    first, second, slot = routing(ids_ref[0, 0:1], ids_ref[0, 1:2], lax.axis_index("expert"))
    last = len(backs)
    place_ref[...] = placing(slot, last, 0).astype(BF)
    gates = [column(weight_ref[0, j : j + 1]) for j in range(2)]
    share = jnp.where(first == last, gates[0], 0.0) + jnp.where(second == last, gates[1], 0.0)
    share_ref[...] = jnp.broadcast_to(share, share_ref.shape)


def grad_kernel(in_ref, att_ref, gain_ref, up_ref, sum_ref, rms_ref, place_ref, share_ref, back_ref, out_hbm, *refs):
    gained_ref, out_ref, sems = refs
    tok, width = in_ref.shape[1], in_ref.shape[2]
    step = 512
    place, share = place_ref[:, : back_ref.shape[0]], share_ref[:, 0:1]
    cross = jnp.zeros((tok, 1), F32)
    for n in range(width // step):
        at = slice(n * step, (n + 1) * step)
        resid = in_ref[0, :, at].astype(F32) + att_ref[:, at].astype(F32)
        gained = gain_ref[:, at] * (sum_ref[:, at] + share * dot(place, back_ref[:, at]))
        gained_ref[:, at] = gained
        cross = cross + (resid * gained).sum(axis=1, keepdims=True)
    inv_rms = rms_ref[:, 0:1]
    pull = inv_rms * inv_rms * inv_rms * (cross / width)
    copies = []
    for n in range(width // step):
        at = slice(n * step, (n + 1) * step)
        resid = in_ref[0, :, at].astype(F32) + att_ref[:, at].astype(F32)
        out_ref[:, at] = (up_ref[0, :, at].astype(F32) + inv_rms * gained_ref[:, at] - resid * pull).astype(BF)
        copies.append(pltpu.make_async_copy(out_ref.at[:, at], out_hbm.at[0, :, at], sems.at[n]))
        copies[-1].start()
    for copy in copies:
        copy.wait()


def shards(
    inputs, queries, keys, values, doc_ids, norm_gain, expert_ids, gate_weights, w_gate, w_up, w_down, out_grad
):
    tok, width = inputs.shape[1], inputs.shape[2]
    hidden_count = w_gate.shape[2]
    peers = lax.axis_size("expert")
    slots = 5 * tok // (2 * peers)
    slots = -(-slots // 16) * 16
    pieces = lax.axis_size("fsdp") * lax.axis_size("ctx")
    total = peers * slots
    slab = jax.ShapeDtypeStruct((slots, width), BF)
    slabs = [slab] * peers
    gain = norm_gain.reshape(1, width)
    ids, gates = jnp.swapaxes(expert_ids, 1, 2), jnp.swapaxes(gate_weights, 1, 2)


    def call(kernel, name, out_shape, count, scratch=(), mib=24):
        return pl.pallas_call(
            kernel,
            out_shape=out_shape,
            in_specs=[VM] * count,
            out_specs=[VM] * len(out_shape) if isinstance(out_shape, list) else VM,
            scratch_shapes=list(scratch),
            compiler_params=params(mib),
            name=name,
        )

    def exchanged(blocks):
        return [block if k == 0 else swapped(block, "expert", k) for k, block in enumerate(blocks)]

    def over_core(block):
        return swapped(block, "ctx", 1)

    def over_x(block):
        return [swapped(block, "fsdp", dx) for dx in range(1, lax.axis_size("fsdp"))]

    both = jnp.pad(keys, ((0, 0), (0, 0), (0, width))) + jnp.pad(values, ((0, 0), (0, 0), (width, 0)))
    previous = shifted(both, ("expert", "ctx"), 1)
    own_others = pl.pallas_call(
        prepare_kernel,
        out_shape=jax.ShapeDtypeStruct((2, w_gate.shape[1], hidden_count), BF),
        in_specs=[pl.BlockSpec(memory_space=pl.ANY)] * 2,
        out_specs=pl.BlockSpec(memory_space=pl.ANY),
        scratch_shapes=[
            pltpu.VMEM((2, w_gate.shape[1], hidden_count), BF),
            pltpu.VMEM(w_down.shape[1:], BF),
            pltpu.SemaphoreType.DMA((4,)),
        ],
        compiler_params=params(56),
        name="prepare",
    )(w_up, after(w_down, both))
    sent_grads = call(lambda *refs: pack_kernel(slots, *refs), "pack_grad", slabs, 2)(ids, after(out_grad, own_others))
    grads = [
        block if k < 2 else swapped(after(block, previous), "expert", k) for k, block in enumerate(sent_grads[:-1])
    ]
    gates_x, others_x = over_x(w_gate), over_x(own_others)

    parts = 2
    cut = width // parts

    def by_part(*dims):
        return pl.BlockSpec((*dims, cut), lambda n: (0,) * len(dims) + (n,))

    def fixed(*dims):
        return pl.BlockSpec(dims, lambda n: (0,) * len(dims))

    attended, *sent_rows = pl.pallas_call(
        lambda *refs: attend_kernel(slots, *refs),
        out_shape=[jax.ShapeDtypeStruct((tok, width), BF)] + slabs,
        grid=(parts,),
        in_specs=[by_part(1, tok)] * 3
        + [by_part(1, tok), pl.BlockSpec((1, tok, cut), lambda n: (0, 0, n + parts)), fixed(*doc_ids.shape), by_part(1, tok), fixed(1, width), fixed(*ids.shape)],
        out_specs=[by_part(tok)] + [fixed(slots, width)] * peers,
        scratch_shapes=[pltpu.VMEM((parts, tok, cut), F32), pltpu.VMEM((tok, HD), F32)],
        compiler_params=params(16),
        name="attend",
    )(queries, keys, values, previous, previous, doc_ids, inputs, gain, ids)
    rows = exchanged([after(block, grads[-1]) if k != peers - 1 else block for k, block in enumerate(sent_rows)])

    all_gates, all_others = [w_gate, over_core(after(w_gate, attended))], [own_others, over_core(after(own_others, attended))]
    for gate, other in zip(gates_x, others_x):
        all_gates += [gate, over_core(after(gate, *rows[1:]))]
        all_others += [other, over_core(after(other, *rows[1:]))]
    grads.append(swapped(after(sent_grads[-1], rows[1]), "expert", peers - 1))

    wide = jax.ShapeDtypeStruct((total, hidden_count), F32)
    x_scratch = pltpu.VMEM((pieces, total, w_gate.shape[1]), BF)
    hidden, slope, silu = call(
        lambda *refs: hidden_kernel(peers, pieces, *refs),
        "hidden",
        [jax.ShapeDtypeStruct((total, hidden_count), BF), wide, wide],
        peers + 2 * pieces,
        [x_scratch],
    )(*rows, *all_gates, *all_others)
    grads[1] = swapped(after(grads[1], hidden), "expert", 1)
    served_out = call(lambda *refs: out_kernel(pieces, *refs), "served", slabs, 1 + pieces)(hidden, *all_others)
    back_out = exchanged(served_out)

    served_grad = call(
        lambda *refs: backward_kernel(len(grads), pieces, slots, *refs),
        "backward",
        slabs,
        len(grads) + 2 * pieces + 2,
        [x_scratch] + [pltpu.VMEM((total, hidden_count), BF)] * 2,
    )(*grads, *all_gates, *all_others, slope, silu)
    back_grad = exchanged(served_grad)

    out_block = jax.ShapeDtypeStruct(inputs.shape, BF)
    layer_out = pl.pallas_call(
        layer_kernel,
        out_shape=out_block,
        in_specs=[VM] * (4 + peers),
        out_specs=VM,
        compiler_params=params(32),
        name="layer",
    )(ids, gates, inputs, attended, *back_out)
    flat = jax.ShapeDtypeStruct((tok, 128), F32)
    near_sum, inv_rms, place, share = call(
        near_grad_kernel,
        "near_grad",
        [jax.ShapeDtypeStruct((tok, width), F32), flat, jax.ShapeDtypeStruct((tok, 128), BF), flat],
        3 + peers,
    )(ids, gates, inputs, after(attended, layer_out), *back_grad[:-1])
    input_grad = pl.pallas_call(
        grad_kernel,
        out_shape=out_block,
        in_specs=[VM] * 9,
        out_specs=pl.BlockSpec(memory_space=pl.ANY),
        scratch_shapes=[
            pltpu.VMEM((tok, width), F32),
            pltpu.VMEM((tok, width), BF),
            pltpu.SemaphoreType.DMA((width // 512,)),
        ],
        compiler_params=params(16),
        name="grad",
    )(inputs, attended, gain, out_grad, near_sum, inv_rms, place, share, back_grad[-1])
    return layer_out, input_grad


def solution(mesh):
    rows = P(("groups", "fsdp"), ("expert", "ctx"), None)
    in_specs = (
        rows,
        rows,
        rows,
        rows,
        P(("groups", "fsdp"), None),
        P(),
        rows,
        rows,
        P("expert", ("fsdp", "ctx"), None),
        P("expert", ("fsdp", "ctx"), None),
        P("expert", None, ("fsdp", "ctx")),
        rows,
    )
    return jax.shard_map(shards, mesh=mesh, in_specs=in_specs, out_specs=(rows, rows), check_vma=False)
```
